128 devices in a mesh: dp: 4 (over z_hi, core), blk: 4 (over y), ulys: 8 (over x, z_lo).
Axes of the slice: x: 4, y: 4, z: 4 (z_hi: 2, z_lo: 2; z = z_hi * 2 + z_lo), core: 2. Of those that a mesh axis runs over, the one named last changes fastest.
Arguments:
- tokens: bfloat16 [16384, 1536], P(('dp', 'blk', 'ulys')), may hold values from -6 to 6
- cotangent: bfloat16 [16384, 1536], P(('dp', 'blk', 'ulys')), may hold values from -6 to 6
- routes: int32 [16384, 8], P(('dp', 'blk', 'ulys')), may hold values from 0 to 39, all different within a row; in each aligned block of 128 rows (0 to 127, 128 to 255, ...) at most 48 rows name the same one
- project_in: float32 [1536, 2560], P(('dp', 'blk', 'ulys')), may hold values from -0.5 to 0.5
- project_out: float32 [1536, 1536], P(None, ('dp', 'blk', 'ulys')), may hold values from -1.5 to 1.5
- router_weight: float32 [1536, 40], P(('dp', 'blk', 'ulys')), may hold values from -0.078125 to 0.078125
- norm_gains: float32 [2, 1536], P(None, ('dp', 'blk', 'ulys')), may hold values from 0.5 to 1.5
- expert_up: float32 [40, 1536, 1024], P('ulys', ('dp', 'blk')), may hold values from -0.15625 to 0.15625
- expert_down: float32 [40, 512, 1536], P('ulys', None, ('dp', 'blk')), may hold values from -6 to 6
- project_in_first: float32 [1536, 2560], P(('dp', 'blk', 'ulys'))
- project_in_second: float32 [1536, 2560], P(('dp', 'blk', 'ulys')), as said below
- project_out_first: float32 [1536, 1536], P(None, ('dp', 'blk', 'ulys'))
- project_out_second: float32 [1536, 1536], P(None, ('dp', 'blk', 'ulys')), as said below
- router_weight_first: float32 [1536, 40], P(('dp', 'blk', 'ulys'))
- router_weight_second: float32 [1536, 40], P(('dp', 'blk', 'ulys')), as said below
- norm_gains_first: float32 [2, 1536], P(None, ('dp', 'blk', 'ulys'))
- norm_gains_second: float32 [2, 1536], P(None, ('dp', 'blk', 'ulys')), as said below
- expert_up_first: float32 [40, 1536, 1024], P('ulys', ('dp', 'blk'))
- expert_up_second: float32 [40, 1536, 1024], P('ulys', ('dp', 'blk')), as said below
- expert_down_first: float32 [40, 512, 1536], P('ulys', None, ('dp', 'blk'))
- expert_down_second: float32 [40, 512, 1536], P('ulys', None, ('dp', 'blk')), as said below
Outputs:
- layer_out: float32 [16384, 1536], P(('dp', 'blk', 'ulys'))
- tokens_grad: float32 [16384, 1536], P(('dp', 'blk', 'ulys'))
- project_in_new: float32 [1536, 2560], P(('dp', 'blk', 'ulys'))
- project_in_first_new: float32 [1536, 2560], P(('dp', 'blk', 'ulys'))
- project_in_second_new: float32 [1536, 2560], P(('dp', 'blk', 'ulys'))
- project_out_new: float32 [1536, 1536], P(None, ('dp', 'blk', 'ulys'))
- project_out_first_new: float32 [1536, 1536], P(None, ('dp', 'blk', 'ulys'))
- project_out_second_new: float32 [1536, 1536], P(None, ('dp', 'blk', 'ulys'))
- router_weight_new: float32 [1536, 40], P(('dp', 'blk', 'ulys'))
- router_weight_first_new: float32 [1536, 40], P(('dp', 'blk', 'ulys'))
- router_weight_second_new: float32 [1536, 40], P(('dp', 'blk', 'ulys'))
- norm_gains_new: float32 [2, 1536], P(None, ('dp', 'blk', 'ulys'))
- norm_gains_first_new: float32 [2, 1536], P(None, ('dp', 'blk', 'ulys'))
- norm_gains_second_new: float32 [2, 1536], P(None, ('dp', 'blk', 'ulys'))
- expert_up_new: float32 [40, 1536, 1024], P('ulys', ('dp', 'blk'))
- expert_up_first_new: float32 [40, 1536, 1024], P('ulys', ('dp', 'blk'))
- expert_up_second_new: float32 [40, 1536, 1024], P('ulys', ('dp', 'blk'))
- expert_down_new: float32 [40, 512, 1536], P('ulys', None, ('dp', 'blk'))
- expert_down_first_new: float32 [40, 512, 1536], P('ulys', None, ('dp', 'blk'))
- expert_down_second_new: float32 [40, 512, 1536], P('ulys', None, ('dp', 'blk'))
The draws below stay inside these ranges and needn't reach their ends.
Inputs may be any that keep to these rules, and one draw needn't show every extreme that they name: `routes`: each row names 8 different experts. In each aligned block of 128 rows (the rows of one device) no expert is named more than 48 times, a bound that some block reaches. `project_in_second`: Positive. `project_out_second`: Positive. `router_weight_second`: Positive. `norm_gains_second`: Positive. `expert_up_second`: Positive. `expert_down_second`: Positive.
All inputs are finite; a program needn't handle non-finite values.
Results may differ from the reference program's by a relative error of at most 0.024.
Values may be sent and summed in bfloat16 or wider, within the bound.
No kernel may reach another device: no remote copies, remote signals or barrier semaphores. Data moves between devices by JAX's collectives and lax.ppermute only.
A program may use at most 256 MiB of HBM per device.

```python
import math
import jax
import jax.numpy as jnp
import numpy as np
from jax import lax

D = 1536
HQ = 24
HK = 8
HD = 64
F = 512
EXPERTS = 40
TOPK = 8
TOK_DEV = 128
ADAM_STEP = 10
SEQ = 4096
TOKENS = 16384
QKV = 2560
CAP = 48
N_DP = 4
N_BLK = 4
N_ULYS = 8


beta_one = 0.9


beta_two = 0.95


def first_draw(random_key, extent, spread):
    return spread * (1.0 - beta_one) / beta_one * jax.random.normal(random_key, extent, jnp.float32)


def second_draw(random_key, extent, spread):
    factor = jnp.exp(jax.random.uniform(random_key, extent, jnp.float32, 0.0, 1.3862944))
    return spread * spread * (1.0 - beta_two) / beta_two * factor


def spread_project_in():
    return 0.05 * (D * TOKENS) ** 0.5


def spread_project_out():
    return 0.3 * TOKENS ** 0.5


def spread_router():
    return 0.0165 * (F * D * TOKENS * TOPK / EXPERTS) ** 0.5


def spread_gains():
    return jnp.array([[9.0], [1.5]], jnp.float32) * TOKENS ** 0.5


def spread_expert_up():
    return 0.014 * (D * TOKENS * TOPK / EXPERTS) ** 0.5


def spread_expert_down():
    return 0.0165 * (TOKENS * TOPK / EXPERTS) ** 0.5


def draw_project_in_first(key, part):
    key = jax.random.fold_in(key, 11)
    return first_draw(key, (D, QKV), spread_project_in())


def draw_project_in_second(key, part):
    key = jax.random.fold_in(key, 12)
    return second_draw(key, (D, QKV), spread_project_in())


def draw_project_out_first(key, part):
    key = jax.random.fold_in(key, 21)
    return first_draw(key, (HQ * HD, D), spread_project_out())


def draw_project_out_second(key, part):
    key = jax.random.fold_in(key, 22)
    return second_draw(key, (HQ * HD, D), spread_project_out())


def draw_router_weight_first(key, part):
    key = jax.random.fold_in(key, 31)
    return first_draw(key, (D, EXPERTS), spread_router())


def draw_router_weight_second(key, part):
    key = jax.random.fold_in(key, 32)
    return second_draw(key, (D, EXPERTS), spread_router())


def draw_norm_gains_first(key, part):
    key = jax.random.fold_in(key, 41)
    return first_draw(key, (2, D), spread_gains())


def draw_norm_gains_second(key, part):
    key = jax.random.fold_in(key, 42)
    return second_draw(key, (2, D), spread_gains())


def draw_expert_up_first(key, part):
    key = jax.random.fold_in(key, 51)
    return first_draw(key, (EXPERTS, D, 2 * F), spread_expert_up())


def draw_expert_up_second(key, part):
    key = jax.random.fold_in(key, 52)
    return second_draw(key, (EXPERTS, D, 2 * F), spread_expert_up())


def draw_expert_down_first(key, part):
    key = jax.random.fold_in(key, 61)
    return first_draw(key, (EXPERTS, F, D), spread_expert_down())


def draw_expert_down_second(key, part):
    key = jax.random.fold_in(key, 62)
    return second_draw(key, (EXPERTS, F, D), spread_expert_down())


def shard_levels(own_key, shape, pieces, least, largest):
    level = 1.0
    for axis_at, shards_of in pieces:
        steps = jax.random.uniform(jax.random.fold_in(jax.random.fold_in(own_key, 6), axis_at), (shards_of,), jnp.float32, least / len(pieces), largest / len(pieces))
        level = level * jnp.repeat(jnp.exp(steps), shape[axis_at] // shards_of).reshape((-1,) + (1,) * (len(shape) - 1 - axis_at))
    return level


def routed_block(key, own, number, rows, count, top, reach, lean):
    ranking = jax.random.permutation(key, count)
    heavy_load, common = shares(count, rows * top, reach, lean, True), shares(count, rows * top, reach, lean, False)
    places = jnp.arange(count)

    def named(tallies, turn):
        used = int((tallies > 0).sum())
        fixed = max(1, used // 4)
        passed = fixed + (places - fixed + turn * (used - fixed)) % max(1, count - fixed)
        return jnp.zeros((count,), jnp.int32).at[ranking[jnp.where(places < fixed, places, passed)]].set(jnp.asarray(tallies, jnp.int32))

    tallies = jnp.where(number % 4 == 0, named(heavy_load, number // 4), named(common, number - number // 4 - 1))
    mixed = jax.random.permutation(jax.random.fold_in(own, 3), count)
    giver, taker = mixed[0:count // 2 * 2:2], mixed[1:count // 2 * 2:2]
    room = jnp.minimum(tallies[giver] - 1, reach - tallies[taker]) // 2
    room = jnp.where((giver == ranking[0]) | (taker == ranking[0]) | (tallies[taker] == 0), 0, jnp.maximum(room, 0))
    passed = jax.random.randint(jax.random.fold_in(own, 4), (count // 2,), 0, 1 << 20) % (room + 1)
    tallies = tallies.at[giver].add(-passed).at[taker].add(passed)
    labels = jnp.searchsorted(jnp.cumsum(tallies), jnp.arange(rows * top), side="right").astype(jnp.int32)
    listing = labels.reshape(top, rows).T
    listing = listing[jax.random.permutation(jax.random.fold_in(own, 1), rows)]
    turn = jax.random.randint(jax.random.fold_in(own, 2), (rows, 1), 0, top)
    return jnp.take_along_axis(listing, (jnp.arange(top)[None, :] + turn) % top, axis=1)


def shares(number_of, total, bound, slope, full):
    loads = [(1 << 20) // math.isqrt(rank ** slope) + 1 for rank in range(1, number_of + 1)]
    largest = bound if full else min(bound, max(-(-total // number_of), total * loads[0] // sum(loads)))
    least = 1 if total - largest >= number_of - 1 else 0
    counts, rest = [largest] + [least] * (number_of - 1), total - largest - least * (number_of - 1)
    while rest > 0:
        candidates = [i for i in range(1, number_of) if counts[i] < largest] or [i for i in range(1, number_of) if counts[i] < bound]
        whole, remaining = sum([loads[i] for i in candidates]), rest
        for i in candidates:
            extra = min(bound - counts[i], max(1, remaining * loads[i] // whole), rest)
            counts[i] = counts[i] + extra
            rest = rest - extra
    return np.array(counts)


def gaussian(stream_key, shape, width, bound, pieces=(), kind=jnp.bfloat16):
    entries = jax.random.normal(stream_key, shape, jnp.float32) * width
    if len(pieces) > 0:
        entries = shard_levels(stream_key, shape, pieces, -0.22, 0.18) * entries
    return jnp.clip(entries, min=-bound, max=bound).astype(kind)


def setup_inputs(seed: int = 0) -> dict:
    key_list = jax.random.split(jax.random.key(seed), 22)
    tokens = gaussian(key_list[0], (TOKENS, D), 1.0, 6.0, ((0, 128),))
    cotangent = gaussian(key_list[1], (TOKENS, D), 1.0, 6.0, ((0, 128),))
    routes_keys = jax.random.split(jax.random.fold_in(key_list[2], 1), TOKENS // TOK_DEV)
    routes_turns = jax.random.permutation(jax.random.fold_in(key_list[2], 3), TOKENS // TOK_DEV)
    routes = jax.vmap(lambda own, number: routed_block(jax.random.fold_in(key_list[2], 2), own, number, TOK_DEV, EXPERTS, TOPK, CAP, 2))(routes_keys, routes_turns).reshape((TOKENS, TOPK))
    project_in = gaussian(key_list[3], (D, QKV), (D // 12) ** -0.5, 0.5, ((0, 128),), jnp.float32)
    project_out = gaussian(key_list[4], (HQ * HD, D), 0.25, 1.5, ((1, 128),), jnp.float32)
    router_weight = gaussian(key_list[5], (D, EXPERTS), (4 * D) ** -0.5, 0.078125, ((0, 128),), jnp.float32)
    norm_gains = jnp.clip(1.0 + 0.1 * jax.random.normal(key_list[6], (2, D), jnp.float32), 0.5, 1.5)
    expert_up = gaussian(key_list[7], (EXPERTS, D, 2 * F), D ** -0.5, 0.15625, ((0, 8), (1, 16)), jnp.float32)
    expert_down = gaussian(key_list[8], (EXPERTS, F, D), 1.0, 6.0, ((0, 8), (2, 16)), jnp.float32)
    project_in_first = draw_project_in_first(jax.random.fold_in(key_list[21], 71), 0)
    project_in_second = draw_project_in_second(jax.random.fold_in(key_list[21], 71), 0)
    project_out_first = draw_project_out_first(jax.random.fold_in(key_list[21], 71), 0)
    project_out_second = draw_project_out_second(jax.random.fold_in(key_list[21], 71), 0)
    router_weight_first = draw_router_weight_first(jax.random.fold_in(key_list[21], 71), 0)
    router_weight_second = draw_router_weight_second(jax.random.fold_in(key_list[21], 71), 0)
    norm_gains_first = draw_norm_gains_first(jax.random.fold_in(key_list[21], 71), 0)
    norm_gains_second = draw_norm_gains_second(jax.random.fold_in(key_list[21], 71), 0)
    expert_up_first = draw_expert_up_first(jax.random.fold_in(key_list[21], 71), 0)
    expert_up_second = draw_expert_up_second(jax.random.fold_in(key_list[21], 71), 0)
    expert_down_first = draw_expert_down_first(jax.random.fold_in(key_list[21], 71), 0)
    expert_down_second = draw_expert_down_second(jax.random.fold_in(key_list[21], 71), 0)
    return dict(tokens=tokens, cotangent=cotangent, routes=routes, project_in=project_in, project_out=project_out, router_weight=router_weight, norm_gains=norm_gains, expert_up=expert_up, expert_down=expert_down, project_in_first=project_in_first, project_in_second=project_in_second, project_out_first=project_out_first, project_out_second=project_out_second, router_weight_first=router_weight_first, router_weight_second=router_weight_second, norm_gains_first=norm_gains_first, norm_gains_second=norm_gains_second, expert_up_first=expert_up_first, expert_up_second=expert_up_second, expert_down_first=expert_down_first, expert_down_second=expert_down_second)


highest = lax.Precision.HIGHEST
attention_scale = 0.015625
residual_scale = 0.22
norm_epsilon = 1e-06
rope_base = 10000.0
beta_first = 0.9
beta_second = 0.95
adam_epsilon = 1e-08
weight_decay = 0.1
rate_project_in = 0.2
rate_project_out = 2.0
rate_router = 0.03
rate_gains = 0.5
rate_expert_up = 0.05
rate_expert_down = 2.0

@jax.custom_vjp
def low(v):
    return lax.optimization_barrier(v.astype(jnp.bfloat16)).astype(jnp.float32)

@jax.custom_vjp
def low_back(v):
    return v

def low_keep(v):
    return (low(v), None)

def low_pass(kept, grad):
    return (grad,)

def back_keep(v):
    return (v, None)

def back_low(kept, grad):
    return (low(grad),)
low.defvjp(low_keep, low_pass)
low_back.defvjp(back_keep, back_low)

def rope_tables(positions, head_dim):
    half_dim = head_dim // 2
    frequency = rope_base ** (-jnp.arange(half_dim, dtype=jnp.float32) * 2.0 / head_dim)
    angles = positions.astype(jnp.float32)[:, None] * frequency[None, :]
    angles = jnp.concatenate([angles, angles], axis=1)
    return (jnp.cos(angles), jnp.sin(angles))

def rotate(values, cosine_table, sine_table):
    half_dim = values.shape[-1] // 2
    turned = jnp.concatenate([-values[..., half_dim:], values[..., :half_dim]], axis=-1)
    return values * cosine_table + turned * sine_table

def rms_scale(rows_in):
    return lax.rsqrt(lax.optimization_barrier(jnp.mean(rows_in * rows_in, axis=1, keepdims=True)) + norm_epsilon)

def slot_table(route_rows, expert_count, capacity):
    flat_routes = route_rows.reshape(-1).astype(jnp.int32)
    onehot = (flat_routes[:, None] == jnp.arange(expert_count, dtype=jnp.int32)[None, :]).astype(jnp.int32)
    before = (jnp.cumsum(onehot, axis=0) - onehot).astype(jnp.int32)
    ranks = lax.optimization_barrier(jnp.sum(before * onehot, axis=1)).astype(jnp.int32)
    return (flat_routes * capacity + ranks).astype(jnp.int32)

def layer_forward(params, x_seq, route_seq):
    project_in, project_out, router_weight, norm_gains, expert_up, expert_down = params
    gains_low = low(norm_gains)
    normed = low(x_seq * rms_scale(x_seq) * gains_low[0])
    mixed_rows = low_back(jnp.dot(normed, low(project_in), precision=highest))
    query_width = HQ * HD
    kv_width = HK * HD
    cosine_table, sine_table = rope_tables(jnp.arange(SEQ, dtype=jnp.int32), HD)
    cosine_table = cosine_table[:, None, :]
    sine_table = sine_table[:, None, :]
    queries = rotate(mixed_rows[:, :query_width].reshape(SEQ, HQ, HD), cosine_table, sine_table)
    key_rows = rotate(mixed_rows[:, query_width:query_width + kv_width].reshape(SEQ, HK, HD), cosine_table, sine_table)
    values = mixed_rows[:, query_width + kv_width:].reshape(SEQ, HK, HD)
    queries = low_back(low(queries))
    key_rows = low_back(low(key_rows))
    values = low_back(low(values))
    group_size = HQ // HK
    block_rows = min(512, SEQ)
    block_count = SEQ // block_rows
    grouped = queries.reshape(block_count, block_rows, HK, group_size, HD)
    offsets = jnp.arange(block_count, dtype=jnp.int32) * block_rows
    key_positions = jnp.arange(SEQ, dtype=jnp.int32)

    def attend(pair_in):
        query_block, offset = pair_in
        scores = jnp.einsum('qhgd,khd->hgqk', query_block, key_rows, precision=highest) * attention_scale
        scores = low_back(scores)
        query_positions = offset + jnp.arange(block_rows, dtype=jnp.int32)
        allowed = key_positions[None, :] <= query_positions[:, None]
        scores = jnp.where(allowed, scores, -jnp.inf)
        weights = low(jax.nn.softmax(scores, axis=-1))
        return jnp.einsum('hgqk,khd->qhgd', weights, values, precision=highest)
    outputs = lax.map(jax.checkpoint(attend), (grouped, offsets))
    attended = low_back(low(outputs.reshape(SEQ, query_width)))
    branch = low_back(jnp.dot(attended, low(project_out), precision=highest))
    hidden = x_seq + residual_scale * branch
    normed_ffn = low(hidden * rms_scale(hidden) * gains_low[1])
    logits = jnp.dot(normed_ffn, low(router_weight), precision=highest)
    chosen = jnp.take_along_axis(logits, route_seq, axis=1)
    gate_weights = jax.nn.softmax(chosen, axis=1)
    holders = N_BLK * N_ULYS
    device_routes = route_seq.reshape(holders, TOK_DEV, TOPK)
    slot_of = jax.vmap(lambda route_block: slot_table(route_block, EXPERTS, CAP))(device_routes)
    expert_of = slot_of // CAP
    rank_of = slot_of % CAP
    holder_ids = jnp.arange(holders, dtype=jnp.int32)[:, None]
    slot_index = ((expert_of * holders + holder_ids) * CAP + rank_of).reshape(-1).astype(jnp.int32)
    token_index = (jnp.arange(SEQ * TOPK, dtype=jnp.int32) // TOPK).astype(jnp.int32)
    source = jnp.zeros((EXPERTS * holders * CAP,), jnp.int32).at[slot_index].set(token_index)
    filled = jnp.zeros((EXPERTS * holders * CAP,), jnp.float32).at[slot_index].set(1.0)
    gathered = low_back(normed_ffn[source] * filled[:, None])
    per_expert = gathered.reshape(EXPERTS, holders * CAP, D)

    def expert_apply(triple):
        rows_in, up_weight, down_weight = triple
        both_parts = low_back(jnp.dot(rows_in, up_weight, precision=highest))
        activated = low(jax.nn.silu(both_parts[:, :F]) * both_parts[:, F:])
        return low_back(low(jnp.dot(activated, down_weight, precision=highest)))
    returned = lax.map(jax.checkpoint(expert_apply), (per_expert, low(expert_up), low(expert_down)))
    picked = returned.reshape(EXPERTS * holders * CAP, D)[slot_index].reshape(SEQ, TOPK, D)
    mixture = lax.optimization_barrier(jnp.sum(gate_weights[:, :, None] * picked, axis=1))
    return hidden + residual_scale * mixture

def adam_update(weight, first_moment, second, gradient, step_rate):
    first_new = beta_first * first_moment + (1.0 - beta_first) * gradient
    second_new = beta_second * second + (1.0 - beta_second) * gradient * gradient
    first_hat = first_new / (1.0 - beta_first ** ADAM_STEP)
    second_hat = second_new / (1.0 - beta_second ** ADAM_STEP)
    weight_new = weight - step_rate * (first_hat / (jnp.sqrt(second_hat) + adam_epsilon) + weight_decay * weight)
    return (weight_new, first_new, second_new)

def reference(tokens, cotangent, routes, project_in, project_out, router_weight, norm_gains, expert_up, expert_down, project_in_first, project_in_second, project_out_first, project_out_second, router_weight_first, router_weight_second, norm_gains_first, norm_gains_second, expert_up_first, expert_up_second, expert_down_first, expert_down_second):
    params = (project_in, project_out, router_weight, norm_gains, expert_up, expert_down)
    token_seqs = tokens.astype(jnp.float32).reshape(N_DP, SEQ, D)
    cotangent_seqs = cotangent.astype(jnp.float32).reshape(N_DP, SEQ, D)
    route_seqs = routes.reshape(N_DP, SEQ, TOPK)

    def per_sequence(totals, triple):
        x_seq, cotangent_seq, route_seq = triple
        out_seq, pullback = jax.vjp(lambda weight_tree, token_seq: layer_forward(weight_tree, token_seq, route_seq), params, x_seq)
        grad_params, grad_tokens = pullback(cotangent_seq)
        totals = jax.tree.map(lambda tree_left, tree_right: tree_left + tree_right, totals, grad_params)
        return (totals, (out_seq, grad_tokens))
    zero_tree = jax.tree.map(jnp.zeros_like, params)
    grads, (out_seqs, grad_seqs) = lax.scan(per_sequence, zero_tree, (token_seqs, cotangent_seqs, route_seqs))
    in_new, in_first, in_second = adam_update(project_in, project_in_first, project_in_second, grads[0], rate_project_in)
    out_new, out_first, out_second = adam_update(project_out, project_out_first, project_out_second, grads[1], rate_project_out)
    router_new, router_first, router_second = adam_update(router_weight, router_weight_first, router_weight_second, grads[2], rate_router)
    gains_new, gains_first, gains_second = adam_update(norm_gains, norm_gains_first, norm_gains_second, grads[3], rate_gains)
    up_new, up_first, up_second = adam_update(expert_up, expert_up_first, expert_up_second, grads[4], rate_expert_up)
    down_new, down_first, down_second = adam_update(expert_down, expert_down_first, expert_down_second, grads[5], rate_expert_down)
    return (out_seqs.reshape(TOKENS, D), grad_seqs.reshape(TOKENS, D), in_new, in_first, in_second, out_new, out_first, out_second, router_new, router_first, router_second, gains_new, gains_first, gains_second, up_new, up_first, up_second, down_new, down_first, down_second)
```

```python
import functools

import jax
import jax.numpy as jnp
from jax import lax
from jax.experimental import pallas as pl
from jax.experimental.pallas import tpu as pltpu
from jax.sharding import Mesh
from jax.sharding import PartitionSpec as P

D = 1536
HQ = 24
HK = 8
HD = 64
F = 512
EXPERTS = 40
TOPK = 8
ADAM_STEP = 10
CAP = 48
TOK = 128
GROUP = 8
LOCAL_E = 5
SPAN = 1024
CHUNK = 512
QW = 192
SLOTS = GROUP * CAP
HALF = HD // 2
EXTRA = 128

bf16 = jnp.bfloat16
f32 = jnp.float32
attention_scale = 0.015625
residual_scale = 0.22
norm_epsilon = 1e-06
rope_base = 10000.0
beta_first = 0.9
beta_second = 0.95
adam_epsilon = 1e-08
weight_decay = 0.1
rate_project_in = 0.2
rate_project_out = 2.0
rate_router = 0.03
rate_gains = 0.5
rate_expert_up = 0.05
rate_expert_down = 2.0
log2_e = 1.4426950408889634

ULYS = ("x", "zl")
ALL = ("zh", "co", "blk", "x", "zl")
DPBLK = ("zh", "co", "blk")


def dot(a, b, dims):
    return lax.dot_general(a, b, ((dims[0], dims[1]), ((), ())), preferred_element_type=f32)


def rms_scale(rows_in):
    return lax.rsqrt(jnp.mean(rows_in * rows_in, axis=1, keepdims=True) + norm_epsilon)


def norm_back(rows_in, scale_in, gain_in, grad_in):
    weighted = grad_in * gain_in
    inner_sum = jnp.mean(weighted * rows_in, axis=1, keepdims=True)
    return scale_in * weighted - rows_in * (scale_in * scale_in * scale_in) * inner_sum


def adam_update(weight, first_moment, second, gradient, step_rate):
    first_new = beta_first * first_moment + (1.0 - beta_first) * gradient
    second_new = beta_second * second + (1.0 - beta_second) * gradient * gradient
    first_hat = first_new / (1.0 - beta_first**ADAM_STEP)
    second_hat = second_new / (1.0 - beta_second**ADAM_STEP)
    weight_new = weight - step_rate * (
        first_hat / (jnp.sqrt(second_hat) + adam_epsilon) + weight_decay * weight
    )
    return (weight_new, first_new, second_new)


def a2a(value, axes):
    return lax.all_to_all(value, axes, split_axis=0, concat_axis=0, tiled=True)


def swap(value, axis):
    return lax.ppermute(value, axis, [(0, 1), (1, 0)])


def zigzag(value):
    pairs = []
    for blk in range(4):
        for x in range(4):
            other = 3 - blk if x >= 2 else blk
            pairs.append((blk * 4 + x, other * 4 + x))
    return lax.ppermute(value, ("blk", "x"), pairs)


def gather_group(value):
    pair = jnp.stack([value, swap(value, "zl")])
    return a2a(jnp.broadcast_to(pair[None], (4,) + pair.shape), "x")


def scatter_group(partial):
    arrived = jnp.sum(a2a(partial, "x").astype(f32), axis=0)
    return arrived[0] + swap(arrived[1].astype(bf16), "zl").astype(f32)


def gather_rows(value):
    mine = a2a(jnp.broadcast_to(value[None], (8,) + value.shape), ("zh", "blk"))
    other = swap(mine, "co")
    first = lax.axis_index("co") == 0
    low = jnp.where(first, mine, other).reshape(2, 1, 4, *value.shape)
    high = jnp.where(first, other, mine).reshape(2, 1, 4, *value.shape)
    return jnp.concatenate([low, high], axis=1).reshape(D, value.shape[1])


def scatter_rows(partial):
    columns = partial.shape[1]
    cut = partial.reshape(2, 2, 4, 96, columns)
    first = lax.axis_index("co") == 0
    keep = jnp.where(first, cut[:, 0], cut[:, 1])
    give = jnp.where(first, cut[:, 1], cut[:, 0])
    both = keep.astype(f32) + swap(give, "co").astype(f32)
    arrived = a2a(both.astype(bf16).reshape(8, 96, columns), ("zh", "blk"))
    return jnp.sum(arrived.astype(f32), axis=0)


def attend_kernel(block_ref, pos_row, pos_col, q_ref, k_ref, v_ref, out_ref, log_ref, acc, peak, total):
    base = 2 * block_ref[0]

    def part(half, at, masked):
        cols = slice(half * CHUNK, (half + 1) * CHUNK)
        keys = k_ref[at]
        vals = v_ref[at]
        for head in range(3):
            scores = dot(keys, q_ref[head, :, cols], ((1,), (0,))) * (attention_scale * log2_e)
            if masked:
                scores = jnp.where(pos_col[...] <= pos_row[...], scores, -jnp.inf)
            before = peak[head]
            now = jnp.maximum(before, jnp.max(scores, axis=0, keepdims=True))
            weights = jnp.exp2(scores - now)
            fade = jnp.exp2(before - now)
            total[head] = total[head] * fade + jnp.sum(weights, axis=0, keepdims=True)
            acc[head] = acc[head] * fade + dot(vals, weights.astype(bf16), ((1,), (0,)))
            peak[head] = now

    for half in range(2):
        cols = slice(half * CHUNK, (half + 1) * CHUNK)
        last = base if half == 0 else 7 - base
        acc[...] = jnp.zeros_like(acc)
        total[...] = jnp.zeros_like(total)
        peak[...] = jnp.full_like(peak, -1e30)
        part(half, last, True)

        def step(at, carry):
            part(half, at, False)
            return carry

        lax.fori_loop(0, last, step, 0)
        for head in range(3):
            out_ref[head, :, cols] = acc[head] / total[head]
            log_ref[head, :, cols] = peak[head] + jnp.log2(total[head])


def attend(block, pos, q_t, keys, vals_t):
    vmem = pl.BlockSpec(memory_space=pltpu.VMEM)
    return pl.pallas_call(
        attend_kernel,
        out_shape=(
            jax.ShapeDtypeStruct((3, HD, SPAN), f32),
            jax.ShapeDtypeStruct((3, 1, SPAN), f32),
        ),
        in_specs=[pl.BlockSpec(memory_space=pltpu.SMEM)] + [vmem] * 5,
        out_specs=(vmem, vmem),
        scratch_shapes=[
            pltpu.VMEM((3, HD, CHUNK), f32),
            pltpu.VMEM((3, 1, CHUNK), f32),
            pltpu.VMEM((3, 1, CHUNK), f32),
        ],
        compiler_params=pltpu.CompilerParams(vmem_limit_bytes=48 << 20),
        cost_estimate=pl.CostEstimate(flops=4 * 9 * 3 * 512 * 512 * 256, bytes_accessed=4 << 20, transcendentals=7 << 20),
        name="attend",
    )(block, pos[None, :], pos[:, None], q_t, keys, vals_t)


def attend_back_kernel(
    block_ref, pos_row, pos_col, qt_ref, q_ref, k_ref, kt_ref, v_ref, dot_ref, do_ref, out_ref, log_ref,
    dq_ref, dk_ref, dv_ref, dq_acc, dk_acc, dv_acc, inner
):
    base = 2 * block_ref[0]
    dk_acc[...] = jnp.zeros_like(dk_acc)
    dv_acc[...] = jnp.zeros_like(dv_acc)
    for head in range(3):
        inner[head] = jnp.sum(dot_ref[head].astype(f32) * out_ref[head], axis=0, keepdims=True)

    def part(half, at, masked):
        cols = slice(half * CHUNK, (half + 1) * CHUNK)
        keys = k_ref[at]
        keys_t = kt_ref[at]
        vals = v_ref[at]
        for head in range(3):
            scores = dot(keys, qt_ref[head, :, cols], ((1,), (0,))) * (attention_scale * log2_e)
            probs = jnp.exp2(scores - log_ref[head, :, cols])
            if masked:
                probs = jnp.where(pos_col[...] <= pos_row[...], probs, 0.0)
            prob_grad = dot(vals, dot_ref[head, :, cols], ((1,), (0,)))
            score_grad = (probs * (prob_grad - inner[head, :, cols])).astype(bf16)
            dv_acc[at] += dot(probs.astype(bf16), do_ref[head, cols], ((1,), (0,)))
            dk_acc[at] += dot(score_grad, q_ref[head, cols], ((1,), (0,)))
            dq_acc[head] += dot(keys_t, score_grad, ((1,), (0,)))

    for half in range(2):
        cols = slice(half * CHUNK, (half + 1) * CHUNK)
        last = base if half == 0 else 7 - base
        dq_acc[...] = jnp.zeros_like(dq_acc)
        part(half, last, True)

        def step(at, carry):
            part(half, at, False)
            return carry

        lax.fori_loop(0, last, step, 0)
        dq_ref[:, :, cols] = (dq_acc[...] * attention_scale).astype(bf16)
    dk_ref[...] = (dk_acc[...] * attention_scale).astype(bf16)
    dv_ref[...] = dv_acc[...].astype(bf16)


def attend_back(block, pos, q_t, q_n, keys, keys_t, vals, grad_t, grad_n, out_t, logs):
    vmem = pl.BlockSpec(memory_space=pltpu.VMEM)
    return pl.pallas_call(
        attend_back_kernel,
        out_shape=(
            jax.ShapeDtypeStruct((3, HD, SPAN), bf16),
            jax.ShapeDtypeStruct((8, CHUNK, HD), bf16),
            jax.ShapeDtypeStruct((8, CHUNK, HD), bf16),
        ),
        in_specs=[pl.BlockSpec(memory_space=pltpu.SMEM)] + [vmem] * 11,
        out_specs=(vmem, vmem, vmem),
        scratch_shapes=[
            pltpu.VMEM((3, HD, CHUNK), f32),
            pltpu.VMEM((8, CHUNK, HD), f32),
            pltpu.VMEM((8, CHUNK, HD), f32),
            pltpu.VMEM((3, 1, SPAN), f32),
        ],
        compiler_params=pltpu.CompilerParams(vmem_limit_bytes=48 << 20),
        cost_estimate=pl.CostEstimate(flops=10 * 9 * 3 * 512 * 512 * 256, bytes_accessed=8 << 20, transcendentals=7 << 20),
        name="attend_back",
    )(block, pos[None, :], pos[:, None], q_t, q_n, keys, keys_t, vals, grad_t, grad_n, out_t, logs)


def pick_rows(rank_ref, at):
    return rank_ref[0, at : at + 1, :] == lax.broadcasted_iota(jnp.int32, (CAP, TOK), 0)


def expert_kernel(
    first_ref, rank_ref, gate_ref, x_ref, c_ref, w_ref,
    sum_ref, rows_ref, slot_ref, act_ref, both_ref, scale_ref, acc
):
    number = pl.program_id(0)
    weights = w_ref.at[:, 0]

    @pl.when(number == 0)
    def _():
        acc[...] = jnp.zeros_like(acc)

    cots = []
    for at in range(GROUP):
        rows = slice(at * CAP, (at + 1) * CAP)
        hits = pick_rows(rank_ref, at)
        onehot = hits.astype(f32).astype(bf16)
        rows_ref[0, rows] = dot(onehot, x_ref[at], ((1,), (0,))).astype(bf16)
        scale = jnp.sum(jnp.where(hits, gate_ref[0, at : at + 1, :], 0.0), axis=1, keepdims=True)
        scale_ref[0, rows] = jnp.broadcast_to(scale, (CAP, 128))
        cot = dot(onehot, c_ref[at, :, :D], ((1,), (0,))) * residual_scale
        slot_ref[0, rows] = (cot * scale).astype(bf16)
    up = weights[:, :, : 2 * F].reshape(D, 2 * F)
    down = weights[:, :, 2 * F :].reshape(D, F)
    both = dot(rows_ref[0], up, ((1,), (0,)))
    gate = both[:, :F]
    linear = both[:, F:]
    sigmoid = 1.0 / (1.0 + jnp.exp(-gate))
    silu = gate * sigmoid
    activated = (silu * linear).astype(bf16)
    act_ref[0] = activated
    slope = sigmoid * (1.0 + gate * (1.0 - sigmoid))
    act_grad = dot(slot_ref[0], down, ((1,), (0,)))
    weighted = jnp.sum(activated.astype(f32) * act_grad, axis=1, keepdims=True)
    both_ref[0, :, :F] = (act_grad * linear * slope).astype(bf16)
    both_ref[0, :, F:] = (act_grad * silu).astype(bf16)
    back = dot(both_ref[0], up, ((1,), (1,))).astype(bf16)
    high = weighted.astype(bf16).astype(f32)
    low = weighted - high
    lane = lax.broadcasted_iota(jnp.int32, (SLOTS, EXTRA), 1)
    mine = first_ref[0] + number
    tail = (jnp.where(lane == mine, high, 0.0) + jnp.where(lane == mine + EXPERTS, low, 0.0)).astype(bf16)
    for at in range(GROUP):
        rows = slice(at * CAP, (at + 1) * CAP)
        onehot = pick_rows(rank_ref, at).astype(f32).astype(bf16)
        acc[at, :, :D] += dot(onehot, back[rows], ((0,), (0,)))
        acc[at, :, D:] += dot(onehot, tail[rows], ((0,), (0,)))

    @pl.when(number == LOCAL_E - 1)
    def _():
        sum_ref[...] = acc[...].astype(bf16)


def expert_pass(first, ranks, gates, rows, cots, weights):
    whole = lambda *shape: pl.BlockSpec(shape, lambda e: (0,) * len(shape), pipeline_mode=pl.Buffered(1))
    return pl.pallas_call(
        expert_kernel,
        grid=(LOCAL_E,),
        out_shape=(
            jax.ShapeDtypeStruct((GROUP, TOK, D + EXTRA), bf16),
            jax.ShapeDtypeStruct((LOCAL_E, SLOTS, D), bf16),
            jax.ShapeDtypeStruct((LOCAL_E, SLOTS, D), bf16),
            jax.ShapeDtypeStruct((LOCAL_E, SLOTS, F), bf16),
            jax.ShapeDtypeStruct((LOCAL_E, SLOTS, 2 * F), bf16),
            jax.ShapeDtypeStruct((LOCAL_E, SLOTS, 128), f32),
        ),
        in_specs=[
            pl.BlockSpec(memory_space=pltpu.SMEM),
            pl.BlockSpec((1, GROUP, TOK), lambda e: (e, 0, 0)),
            pl.BlockSpec((1, GROUP, TOK), lambda e: (e, 0, 0)),
            whole(GROUP, TOK, D),
            whole(GROUP, TOK, D + EXTRA),
            pl.BlockSpec((16, 1, 96, 3 * F), lambda e: (0, e, 0, 0)),
        ],
        out_specs=(
            whole(GROUP, TOK, D + EXTRA),
            pl.BlockSpec((1, SLOTS, D), lambda e: (e, 0, 0)),
            pl.BlockSpec((1, SLOTS, D), lambda e: (e, 0, 0)),
            pl.BlockSpec((1, SLOTS, F), lambda e: (e, 0, 0)),
            pl.BlockSpec((1, SLOTS, 2 * F), lambda e: (e, 0, 0)),
            pl.BlockSpec((1, SLOTS, 128), lambda e: (e, 0, 0)),
        ),
        scratch_shapes=[pltpu.VMEM((GROUP, TOK, D + EXTRA), f32)],
        compiler_params=pltpu.CompilerParams(vmem_limit_bytes=58 << 20),
        cost_estimate=pl.CostEstimate(flops=5 * 3 * 10**9, bytes_accessed=60 << 20, transcendentals=1 << 20),
        name="experts",
    )(first, ranks, gates, rows, cots, weights)


def grad_kernel(rows_ref, slot_ref, act_ref, both_ref, out_ref):
    for at in range(4):
        cols = slice(at * 384, (at + 1) * 384)
        up = dot(rows_ref[0, :, cols], both_ref[0], ((0,), (0,)))
        out_ref[at * 4 : at * 4 + 4, 0, :, : 2 * F] = up.astype(bf16).reshape(4, 96, 2 * F)
        down = dot(slot_ref[0, :, cols], act_ref[0], ((0,), (0,)))
        out_ref[at * 4 : at * 4 + 4, 0, :, 2 * F :] = down.astype(bf16).reshape(4, 96, F)


def expert_grads(rows, slots, activated, both):
    block = lambda width: pl.BlockSpec((1, SLOTS, width), lambda e: (e, 0, 0))
    return pl.pallas_call(
        grad_kernel,
        grid=(LOCAL_E,),
        out_shape=jax.ShapeDtypeStruct((16, LOCAL_E, 96, 3 * F), bf16),
        in_specs=[block(D), block(D), block(F), block(2 * F)],
        out_specs=pl.BlockSpec((16, 1, 96, 3 * F), lambda e: (0, e, 0, 0)),
        compiler_params=pltpu.CompilerParams(vmem_limit_bytes=48 << 20),
        cost_estimate=pl.CostEstimate(flops=9 * 10**9, bytes_accessed=45 << 20, transcendentals=0),
        name="expert_grads",
    )(rows, slots, activated, both)


def mixture_kernel(rank_ref, act_ref, scale_ref, w_ref, sum_ref, acc):
    number = pl.program_id(0)

    @pl.when(number == 0)
    def _():
        acc[...] = jnp.zeros_like(acc)

    down = w_ref[:, 0].reshape(D, F)
    produced = dot(act_ref[0], down, ((1,), (1,))).astype(bf16).astype(f32)
    produced = (produced * scale_ref[0, :, 0:1]).astype(bf16)
    for at in range(GROUP):
        rows = slice(at * CAP, (at + 1) * CAP)
        onehot = pick_rows(rank_ref, at).astype(f32).astype(bf16)
        acc[at] += dot(onehot, produced[rows], ((0,), (0,)))

    @pl.when(number == LOCAL_E - 1)
    def _():
        sum_ref[...] = acc[...].astype(bf16)


def expert_mixture(ranks, activated, scales, weights):
    return pl.pallas_call(
        mixture_kernel,
        grid=(LOCAL_E,),
        out_shape=jax.ShapeDtypeStruct((GROUP, TOK, D), bf16),
        in_specs=[
            pl.BlockSpec((1, GROUP, TOK), lambda e: (e, 0, 0)),
            pl.BlockSpec((1, SLOTS, F), lambda e: (e, 0, 0)),
            pl.BlockSpec((1, SLOTS, 128), lambda e: (e, 0, 0)),
            pl.BlockSpec((16, 1, 96, F), lambda e: (0, e, 0, 2)),
        ],
        out_specs=pl.BlockSpec((GROUP, TOK, D), lambda e: (0, 0, 0)),
        scratch_shapes=[pltpu.VMEM((GROUP, TOK, D), f32)],
        compiler_params=pltpu.CompilerParams(vmem_limit_bytes=48 << 20),
        cost_estimate=pl.CostEstimate(flops=4 * 10**9, bytes_accessed=20 << 20, transcendentals=0),
        name="mixture",
    )(ranks, activated, scales, weights)


def shards(
    tokens, cotangent, routes, project_in, project_out, router_weight, norm_gains, expert_up, expert_down,
    project_in_first, project_in_second, project_out_first, project_out_second,
    router_weight_first, router_weight_second, norm_gains_first, norm_gains_second,
    expert_up_first, expert_up_second, expert_down_first, expert_down_second,
):
    block = lax.axis_index("blk")
    z_low = lax.axis_index("zl")
    ulys = lax.axis_index("x") * 2 + z_low

    experts_own = jnp.concatenate(
        [expert_up.astype(bf16), jnp.swapaxes(expert_down.astype(bf16), 1, 2)], axis=2
    )
    experts_full = lax.all_gather(
        experts_own.reshape(LOCAL_E * 96, 3 * F), DPBLK, axis=0, tiled=True
    ).reshape(16, LOCAL_E, 96, 3 * F)

    tokens = zigzag(tokens)
    tokens_all = gather_group(tokens).reshape(SPAN, D)

    in_own = project_in.astype(bf16)
    small = jnp.concatenate([router_weight.astype(bf16), norm_gains.astype(bf16).T], axis=1)
    small = jnp.pad(small, ((0, 0), (0, 22)))
    out_own = project_out.astype(bf16).T
    cut = lambda v: jnp.swapaxes(v.reshape(12, GROUP, -1), 0, 1)
    payload = jnp.concatenate(
        [
            cut(in_own[:, :1536]),
            cut(in_own[:, 1536:2048]),
            cut(in_own[:, 2048:]),
            jnp.broadcast_to(small[None], (GROUP, 12, 64)),
            jnp.broadcast_to(out_own[None], (GROUP, 12, D)),
        ],
        axis=2,
    )
    arrived = a2a(payload, ULYS).reshape(96, 384 + D)
    near = gather_rows(arrived[:, :384])
    out_t = gather_rows(arrived[:, 384:])
    in_cols = near[:, :320]
    router_full = near[:, 320:360]
    gains = near[:, 360:362].astype(f32).T
    gain_attn = gains[0]
    gain_ffn = gains[1]

    cotangent = zigzag(cotangent)
    route_cols = zigzag(routes).astype(bf16)
    carried = jnp.concatenate([cotangent, jnp.pad(route_cols, ((0, 0), (0, EXTRA - TOPK)))], axis=1)
    carried_all = gather_group(carried).reshape(GROUP, TOK, D + EXTRA)

    x_all = tokens_all.astype(f32)
    scale_all = rms_scale(x_all)
    normed_all = (x_all * scale_all * gain_attn).astype(bf16)
    mixed_t = dot(in_cols, normed_all, ((0,), (1,)))
    x_of = jnp.arange(SPAN, dtype=jnp.int32) // 256
    turn = jnp.arange(SPAN, dtype=jnp.int32) // 128 % 2
    within = ((x_of % 2) * 2 + (turn ^ z_low)) * 128 + jnp.arange(SPAN, dtype=jnp.int32) % 128
    chunk_of = jnp.where(x_of < 2, 2 * block, 7 - 2 * block)
    position = (chunk_of * CHUNK + within).astype(f32)
    frequency = rope_base ** (-jnp.arange(HALF, dtype=f32) * 2.0 / HD)
    angles = frequency[:, None] * position[None, :]
    cosine = jnp.cos(angles)
    sine = jnp.sin(angles)
    turned = mixed_t[:256].reshape(4, 2, HALF, SPAN)
    lower = turned[:, 0] * cosine - turned[:, 1] * sine
    upper = turned[:, 1] * cosine + turned[:, 0] * sine
    turned = jnp.stack([lower, upper], axis=1).astype(bf16).reshape(4, HD, SPAN)
    q_t = turned[:3]
    kv_t = jnp.concatenate([turned[3], mixed_t[256:].astype(bf16)], axis=0)
    kv_all = a2a(jnp.broadcast_to(kv_t[None], (4, 128, SPAN)), "blk")
    chunks = []
    for at in range(8):
        source, half = (at // 2, 0) if at % 2 == 0 else ((7 - at) // 2, 1)
        chunks.append(kv_all[source, :, half * CHUNK : (half + 1) * CHUNK])
    kv_chunks = jnp.stack(chunks)
    keys_t = kv_chunks[:, :HD]
    vals_t = kv_chunks[:, HD:]
    keys_n = jnp.swapaxes(keys_t, 1, 2)
    vals_n = jnp.swapaxes(vals_t, 1, 2)
    block_one = block.reshape(1).astype(jnp.int32)
    mask_pos = within[:CHUNK]
    heads_t, logs = attend(block_one, mask_pos, q_t, keys_n, vals_t)
    heads_low = heads_t.astype(bf16).reshape(QW, GROUP, TOK)
    absolute = lambda v: jnp.where(z_low == 0, v, v[:, ::-1])
    sent = absolute(jnp.swapaxes(heads_low, 0, 1).reshape(4, 2, QW, TOK)).reshape(GROUP, QW, TOK)
    attended_t = a2a(sent, ULYS).reshape(D, TOK)

    branch = dot(attended_t, out_t, ((0,), (1,)))
    x_own = tokens.astype(f32)
    hidden = x_own + residual_scale * branch
    scale_ffn = rms_scale(hidden)
    normed_ffn = (hidden * scale_ffn * gain_ffn).astype(bf16)
    ffn_all = gather_group(normed_ffn).reshape(GROUP, TOK, D)

    def gates_of(logits, hits):
        masked = jnp.where(hits, logits, -jnp.inf)
        raised = jnp.exp(masked - jnp.max(masked, axis=-1, keepdims=True))
        return raised / jnp.sum(raised, axis=-1, keepdims=True)

    expert_ids = jnp.arange(EXPERTS, dtype=jnp.int32)
    route_all = carried_all[:, :, D : D + TOPK].astype(jnp.int32)
    hits_all = jnp.any(route_all[..., None] == expert_ids, axis=2)
    hits_own = jnp.any(route_cols.astype(jnp.int32)[..., None] == expert_ids, axis=1)
    first = (ulys * LOCAL_E).astype(jnp.int32)
    hits_local = lax.dynamic_slice_in_dim(hits_all, first, LOCAL_E, axis=2)
    earlier = jnp.tril(jnp.ones((TOK, TOK), bf16), -1)
    ranks = jnp.einsum("rt,stj->jsr", earlier, hits_local.astype(bf16), preferred_element_type=f32)
    ranks = jnp.where(jnp.transpose(hits_local, (2, 0, 1)), ranks.astype(jnp.int32), -1)
    logits_all = dot(ffn_all.reshape(SPAN, D), router_full, ((1,), (0,)))
    gates_all = gates_of(logits_all.reshape(GROUP, TOK, EXPERTS), hits_all)
    gates_local = jnp.transpose(lax.dynamic_slice_in_dim(gates_all, first, LOCAL_E, axis=2), (2, 0, 1))
    gates_own = gates_of(dot(normed_ffn, router_full, ((1,), (0,))), hits_own)

    ffn_sums, slot_rows, slot_grads, activated, both_grad, slot_gates = expert_pass(
        first.reshape(1), ranks, gates_local, ffn_all, carried_all, experts_full
    )
    expert_grad = expert_grads(slot_rows, slot_grads, activated, both_grad)
    expert_sum = lax.psum_scatter(
        expert_grad.reshape(16 * LOCAL_E * 96, 3 * F), DPBLK, scatter_dimension=0, tiled=True
    ).reshape(LOCAL_E, 96, 3 * F)
    returned = scatter_group(ffn_sums.reshape(4, 2, TOK, D + EXTRA))

    upstream = cotangent.astype(f32)
    weighted = returned[:, D : D + EXPERTS] + returned[:, D + EXPERTS : D + 2 * EXPERTS]
    logit_grad = weighted - gates_own * jnp.sum(weighted, axis=1, keepdims=True)
    ffn_grad = returned[:, :D] + jnp.dot(
        logit_grad, router_full.astype(f32).T, precision=lax.Precision.HIGHEST
    )
    router_grad = dot(normed_ffn, logit_grad.astype(bf16), ((0,), (0,)))
    gain_ffn_grad = jnp.sum(ffn_grad * hidden * scale_ffn, axis=0)
    hidden_grad = upstream + norm_back(hidden, scale_ffn, gain_ffn, ffn_grad)
    branch_grad = (residual_scale * hidden_grad).astype(bf16)

    attended_grad_t = dot(out_t, branch_grad, ((0,), (1,))).astype(bf16)
    grad_all = a2a(attended_grad_t.reshape(GROUP, QW, TOK), ULYS)
    grad_all = absolute(grad_all.reshape(4, 2, QW, TOK)).reshape(GROUP, QW, TOK)
    grad_t = jnp.swapaxes(grad_all, 0, 1).reshape(3, HD, SPAN)
    dq_t, dk, dv = attend_back(
        block_one, mask_pos, q_t, jnp.swapaxes(q_t, 1, 2), keys_n, keys_t, vals_n,
        grad_t, jnp.swapaxes(grad_t, 1, 2), heads_t, logs,
    )
    kv_grad = jnp.concatenate([dk, dv], axis=2)
    kv_parts = jnp.stack([jnp.concatenate([kv_grad[2 * g], kv_grad[7 - 2 * g]], axis=0) for g in range(4)])
    kv_sum_t = jnp.sum(a2a(kv_parts, "blk").astype(f32), axis=0).T.astype(bf16)

    branch_grad_all = gather_group(branch_grad).reshape(SPAN, D)
    out_grad_t = dot(branch_grad_all, heads_low.reshape(QW, SPAN), ((0,), (1,)))

    mixture_sums = expert_mixture(ranks, activated, slot_gates, experts_full)
    layer_out = hidden + residual_scale * scatter_group(mixture_sums.reshape(4, 2, TOK, D))

    back = jnp.concatenate([dq_t.reshape(QW, SPAN), kv_sum_t[:HD]], axis=0).astype(f32)
    back = back.reshape(4, 2, HALF, SPAN)
    lower = back[:, 0] * cosine + back[:, 1] * sine
    upper = back[:, 1] * cosine - back[:, 0] * sine
    back = jnp.stack([lower, upper], axis=1).astype(bf16).reshape(256, SPAN)
    mixed_grad_t = jnp.concatenate([back, kv_sum_t[HD:]], axis=0)
    in_grad = dot(normed_all, mixed_grad_t, ((0,), (1,)))
    normed_part = dot(mixed_grad_t, in_cols, ((0,), (1,)))
    gain_attn_grad = jnp.sum(normed_part * x_all * scale_all, axis=0)
    normed_grad = scatter_group(normed_part.astype(bf16).reshape(4, 2, TOK, D))
    tokens_grad = hidden_grad + norm_back(x_own, rms_scale(x_own), gain_attn, normed_grad)

    rest = jnp.stack([gain_attn_grad, gain_ffn_grad], axis=1)
    grads = jnp.concatenate(
        [in_grad.astype(bf16), out_grad_t.astype(bf16), router_grad.astype(bf16), rest.astype(bf16)], axis=1
    )
    grads = jnp.pad(grads, ((0, 0), (0, 640 - 554)))
    owned = a2a(scatter_rows(grads).astype(bf16).reshape(GROUP, 12, 640), ULYS).astype(f32)
    lay = lambda v: jnp.swapaxes(v, 0, 1).reshape(12, -1)
    in_sum = jnp.concatenate([lay(owned[:, :, :192]), lay(owned[:, :, 192:256]), lay(owned[:, :, 256:320])], axis=1)
    out_sum = lay(owned[:, :, 320:512]).T
    shared_sum = jnp.sum(owned[:, :, 512:554], axis=0)
    router_sum = shared_sum[:, :EXPERTS]
    gains_sum = shared_sum[:, EXPERTS:].T
    up_sum = expert_sum[:, :, : 2 * F].astype(f32)
    down_sum = jnp.swapaxes(expert_sum[:, :, 2 * F :], 1, 2).astype(f32)

    layer_out = zigzag(layer_out)
    tokens_grad = zigzag(tokens_grad)
    return (
        layer_out,
        tokens_grad,
        *adam_update(project_in, project_in_first, project_in_second, in_sum, rate_project_in),
        *adam_update(project_out, project_out_first, project_out_second, out_sum, rate_project_out),
        *adam_update(router_weight, router_weight_first, router_weight_second, router_sum, rate_router),
        *adam_update(norm_gains, norm_gains_first, norm_gains_second, gains_sum, rate_gains),
        *adam_update(expert_up, expert_up_first, expert_up_second, up_sum, rate_expert_up),
        *adam_update(expert_down, expert_down_first, expert_down_second, down_sum, rate_expert_down),
    )


def solution(mesh):
    fine = Mesh(mesh.devices.reshape(2, 2, 4, 4, 2), ALL)
    rows = P(ALL, None)
    cols = P(None, ALL)
    up = P(ULYS, DPBLK, None)
    down = P(ULYS, None, DPBLK)
    in_specs = (rows,) * 4 + (cols, rows, cols, up, down)
    in_specs += (rows,) * 2 + (cols,) * 2 + (rows,) * 2 + (cols,) * 2 + (up,) * 2 + (down,) * 2
    out_specs = (rows,) * 5 + (cols,) * 3 + (rows,) * 3 + (cols,) * 3 + (up,) * 3 + (down,) * 3
    return jax.shard_map(shards, mesh=fine, in_specs=in_specs, out_specs=out_specs, check_vma=False)
```

```python
import functools

import jax
import jax.numpy as jnp
from jax import lax
from jax.experimental import pallas as pl
from jax.experimental.pallas import tpu as pltpu
from jax.sharding import Mesh
from jax.sharding import PartitionSpec as P

D = 1536
HQ = 24
HK = 8
HD = 64
F = 512
EXPERTS = 40
TOPK = 8
ADAM_STEP = 10
CAP = 48
TOK = 128
GROUP = 8
LOCAL_E = 5
SPAN = 1024
ROWS = 80
CHUNK = 512
QW = 192
SLOTS = GROUP * CAP
HALF = HD // 2
EXTRA = 128
VMEM_LIMIT = 60 << 20
WIDE = 640
ROUTER_AT = 64
GAIN_AT = 104

bf16 = jnp.bfloat16
f32 = jnp.float32
attention_scale = 0.015625
residual_scale = 0.22
norm_epsilon = 1e-06
rope_base = 10000.0
beta_first = 0.9
beta_second = 0.95
adam_epsilon = 1e-08
weight_decay = 0.1
rate_project_in = 0.2
rate_project_out = 2.0
rate_router = 0.03
rate_gains = 0.5
rate_expert_up = 0.05
rate_expert_down = 2.0
log2_e = 1.4426950408889634

ULYS = ("x", "zl")
ALL = ("zh", "co", "blk", "x", "zl")
DPBLK = ("zh", "co", "blk")


def dot(a, b, dims):
    return lax.dot_general(a, b, ((dims[0], dims[1]), ((), ())), preferred_element_type=f32)


def rms_scale(rows_in):
    return lax.rsqrt(jnp.mean(rows_in * rows_in, axis=1, keepdims=True) + norm_epsilon)


def norm_back(rows_in, scale_in, gain_in, grad_in):
    weighted = grad_in * gain_in
    inner_sum = jnp.mean(weighted * rows_in, axis=1, keepdims=True)
    return scale_in * weighted - rows_in * (scale_in * scale_in * scale_in) * inner_sum


def adam_update(weight, first_moment, second, gradient, step_rate):
    first_new = beta_first * first_moment + (1.0 - beta_first) * gradient
    second_new = beta_second * second + (1.0 - beta_second) * gradient * gradient
    first_hat = first_new / (1.0 - beta_first**ADAM_STEP)
    second_hat = second_new / (1.0 - beta_second**ADAM_STEP)
    weight_new = weight - step_rate * (
        first_hat / (jnp.sqrt(second_hat) + adam_epsilon) + weight_decay * weight
    )
    return (weight_new, first_new, second_new)


def a2a(value, axes):
    return lax.all_to_all(value, axes, split_axis=0, concat_axis=0, tiled=True)


def trade(value, axis, mask):
    return lax.ppermute(value, axis, [(i, i ^ mask) for i in range(2 if axis in ("zl", "co", "zh") else 4)])


def after(value, *others):
    return lax.optimization_barrier((value,) + others)[0]


def spread(near, partner):
    a0 = trade(near, "x", 1)
    b0 = trade(near, "x", 3)
    far0 = trade(near, "x", 2)
    b1 = trade(partner, "x", 3)
    a1 = trade(partner, "x", 1)
    far1 = trade(partner, "x", 2)
    return [near, partner, a0, a1, far0, far1, b0, b1]


def collect(blocks, gate=None, last=None):
    to3 = trade(blocks[5], "x", 3)
    to1 = trade(blocks[4], "x", 1)
    got3_1 = trade(blocks[7], "x", 3)
    got1_0 = trade(blocks[2], "x", 1)
    if gate is not None:
        to3, to1, _ = lax.optimization_barrier((to3, to1, gate))
    send1 = (blocks[3].astype(f32) + to3.astype(f32)).astype(bf16)
    send3 = (blocks[6].astype(f32) + to1.astype(f32)).astype(bf16)
    got1_1 = trade(send1, "x", 1)
    got3_0 = trade(send3, "x", 3)
    if last is not None:
        got1_1 = after(got1_1, last)
    other = (blocks[1].astype(f32) + got1_1.astype(f32) + got3_1.astype(f32)).astype(bf16)
    other = trade(other, "zl", 1)
    return (blocks[0], got1_0, got3_0, other)


def total_of(parts):
    return sum(part.astype(f32) for part in parts)


def vmem_specs(count):
    return [pl.BlockSpec(memory_space=pltpu.VMEM)] * count


NO_COST = pl.CostEstimate(flops=0, bytes_accessed=0, transcendentals=0)
SCALARS = pl.BlockSpec(memory_space=pltpu.SMEM)


def project_kernel(info_ref, mine_ref, other_ref, cos_ref, sin_ref, *refs):
    xs = refs[:4]
    near_ref, tail_ref, normed_ref, q_ref, kv_ref, mixed = refs[4:]
    for zh in range(2):
        for blk in range(4):
            own = (zh * 2 + info_ref[3]) * 4 + blk
            far = (zh * 2 + 1 - info_ref[3]) * 4 + blk
            near_ref[own] = mine_ref[zh * 4 + blk]
            near_ref[far] = other_ref[zh * 4 + blk]
    near = near_ref[...].reshape(D, WIDE)
    tail_ref[...] = near[:, 512:].astype(f32).T
    gain = tail_ref[GAIN_AT : GAIN_AT + 1, :]
    weights = near[:, : QW + 2 * HD]
    for at in range(GROUP):
        span = slice(at * TOK, (at + 1) * TOK)
        rows = xs[at // 2][at % 2].astype(f32)
        normed = (rows * rms_scale(rows) * gain).astype(bf16)
        normed_ref[span] = normed
        mixed[:, span] = dot(normed, weights, ((1,), (0,))).T
    cosine = cos_ref[...]
    sine = sin_ref[...]
    for head in range(4):
        low = mixed[head * HD : head * HD + HALF]
        high = mixed[head * HD + HALF : (head + 1) * HD]
        low_out = (low * cosine - high * sine).astype(bf16)
        high_out = (high * cosine + low * sine).astype(bf16)
        if head < 3:
            q_ref[head, :HALF] = low_out
            q_ref[head, HALF:] = high_out
        else:
            kv_ref[:HALF] = low_out
            kv_ref[HALF:HD] = high_out
    kv_ref[HD:] = mixed[4 * HD :].astype(bf16)


def project(info, mine, other, cosine, sine, token_pairs):
    return pl.pallas_call(
        project_kernel,
        out_shape=(
            jax.ShapeDtypeStruct((16, 96, WIDE), bf16),
            jax.ShapeDtypeStruct((128, D), f32),
            jax.ShapeDtypeStruct((SPAN, D), bf16),
            jax.ShapeDtypeStruct((3, HD, SPAN), bf16),
            jax.ShapeDtypeStruct((2 * HD, SPAN), bf16),
        ),
        in_specs=[SCALARS] + vmem_specs(8),
        out_specs=tuple(vmem_specs(5)),
        scratch_shapes=[pltpu.VMEM((QW + 2 * HD, SPAN), f32)],
        compiler_params=pltpu.CompilerParams(vmem_limit_bytes=VMEM_LIMIT),
        cost_estimate=NO_COST,
        name="project",
    )(info, mine, other, cosine, sine, *token_pairs)


def chunk_place(info_ref, chunk):
    source = jnp.bitwise_xor(chunk // 2, info_ref[0])
    return source * 2 + jnp.bitwise_xor(chunk % 2, info_ref[1])


def causal_parts(info_ref, part):
    for half in range(2):
        last = 2 * info_ref[0] + jnp.bitwise_xor(half, info_ref[1])
        part(half, half, True)

        def step(chunk, carry):
            part(half, chunk_place(info_ref, chunk), False)
            return carry

        lax.fori_loop(0, last, step, 0)


def attend_kernel(
    info_ref, pos_row, pos_col, q_ref, near_ref, kv0, kv1, kv2, kv3, out_ref, low_ref, log_ref, *refs
):
    branches = refs[:GROUP]
    keys, vals, acc, peak = refs[GROUP:]
    for source, kv in enumerate((kv0, kv1, kv2, kv3)):
        for half in range(2):
            cols = slice(half * CHUNK, (half + 1) * CHUNK)
            keys[source * 2 + half] = kv[:HD, cols].T
            vals[source * 2 + half, :HD] = kv[HD:, cols]
            vals[source * 2 + half, HD:] = jnp.ones((ROWS - HD, CHUNK), bf16)

    def run(follow):
        def part(half, at, masked):
            cols = slice(half * CHUNK, (half + 1) * CHUNK)
            key = keys[at]
            val = vals[at]
            for head in range(3):
                scores = dot(key, q_ref[head, :, cols], ((1,), (0,))) * (attention_scale * log2_e)
                if masked:
                    scores = jnp.where(pos_col[...] <= pos_row[...], scores, -jnp.inf)
                    now = jnp.max(scores, axis=0, keepdims=True)
                elif follow:
                    now = jnp.maximum(peak[head, :, cols], jnp.max(scores, axis=0, keepdims=True))
                else:
                    now = peak[head, :, cols]
                grown = dot(val, jnp.exp2(scores - now).astype(bf16), ((1,), (0,)))
                if masked:
                    acc[head, :, cols] = grown
                elif follow:
                    acc[head, :, cols] = acc[head, :, cols] * jnp.exp2(peak[head, :, cols] - now) + grown
                else:
                    acc[head, :, cols] += grown
                if masked or follow:
                    peak[head, :, cols] = now

        causal_parts(info_ref, part)

    run(False)
    odd = jnp.where(jnp.abs(acc[...]) < 1e37, 0.0, 1.0)

    @pl.when(jnp.sum(odd) > 0.0)
    def _():
        run(True)

    for head in range(3):
        total = acc[head, HD : HD + 1]
        result = acc[head, :HD] / total
        out_ref[head] = result
        log_ref[head] = peak[head] + jnp.log2(total)
        low_ref[head * HD : (head + 1) * HD] = result.astype(bf16)
    out_cols = near_ref[:, :, 384 : 384 + QW].reshape(D, QW)
    for at in range(GROUP):
        heads = low_ref[:, at * TOK : (at + 1) * TOK]
        branches[at][...] = dot(heads, out_cols, ((0,), (1,))).astype(bf16)


def attend(info, pos, q_t, near, kvs):
    return pl.pallas_call(
        attend_kernel,
        out_shape=(
            jax.ShapeDtypeStruct((3, HD, SPAN), f32),
            jax.ShapeDtypeStruct((QW, SPAN), bf16),
            jax.ShapeDtypeStruct((3, 1, SPAN), f32),
        )
        + (jax.ShapeDtypeStruct((TOK, D), bf16),) * GROUP,
        in_specs=[SCALARS] + vmem_specs(8),
        out_specs=tuple(vmem_specs(3 + GROUP)),
        scratch_shapes=[
            pltpu.VMEM((8, CHUNK, HD), bf16),
            pltpu.VMEM((8, ROWS, CHUNK), bf16),
            pltpu.VMEM((3, ROWS, SPAN), f32),
            pltpu.VMEM((3, 1, SPAN), f32),
        ],
        compiler_params=pltpu.CompilerParams(vmem_limit_bytes=VMEM_LIMIT),
        cost_estimate=NO_COST,
        name="attend",
    )(info, pos[None, :], pos[:, None], q_t, near, *kvs)


def attend_back_kernel(
    info_ref, pos_row, pos_col, qt_ref, near_ref, kv0, kv1, kv2, kv3, out_ref, log_ref, *refs
):
    grads = refs[:GROUP]
    dq_ref, dkv0, dkv1, dkv2, dkv3, qn, kn, kt, vn, gt, gn, dq_acc, dk_acc, dv_acc, inner = refs[GROUP:]
    for source, kv in enumerate((kv0, kv1, kv2, kv3)):
        for half in range(2):
            cols = slice(half * CHUNK, (half + 1) * CHUNK)
            kt[source * 2 + half] = kv[:HD, cols]
            kn[source * 2 + half] = kv[:HD, cols].T
            vn[source * 2 + half] = kv[HD:, cols].T
    out_cols = near_ref[:, :, 384 : 384 + QW].reshape(D, QW)
    for at in range(GROUP):
        span = slice(at * TOK, (at + 1) * TOK)
        grad = dot(grads[at][...], out_cols, ((1,), (0,)))
        grad_t = grad.T
        for head in range(3):
            gn[head, span] = grad[:, head * HD : (head + 1) * HD].astype(bf16)
            gt[head, :, span] = grad_t[head * HD : (head + 1) * HD].astype(bf16)
    dk_acc[...] = jnp.zeros_like(dk_acc)
    dv_acc[...] = jnp.zeros_like(dv_acc)
    for head in range(3):
        inner[head] = jnp.sum(gt[head].astype(f32) * out_ref[head], axis=0, keepdims=True)
        qn[head] = qt_ref[head].T

    dq_acc[...] = jnp.zeros_like(dq_acc)

    def part(half, at, masked):
        cols = slice(half * CHUNK, (half + 1) * CHUNK)
        keys = kn[at]
        keys_t = kt[at]
        vals = vn[at]
        for head in range(3):
            scores = dot(keys, qt_ref[head, :, cols], ((1,), (0,))) * (attention_scale * log2_e)
            probs = jnp.exp2(scores - log_ref[head, :, cols])
            if masked:
                probs = jnp.where(pos_col[...] <= pos_row[...], probs, 0.0)
            prob_grad = dot(vals, gt[head, :, cols], ((1,), (0,)))
            score_grad = (probs * (prob_grad - inner[head, :, cols])).astype(bf16)
            dv_acc[at] += dot(probs.astype(bf16), gn[head, cols], ((1,), (0,)))
            dk_acc[at] += dot(score_grad, qn[head, cols], ((1,), (0,)))
            dq_acc[head, :, cols] += dot(keys_t, score_grad, ((1,), (0,)))

    causal_parts(info_ref, part)
    dq_ref[...] = (dq_acc[...] * attention_scale).astype(bf16)
    for source, dkv in enumerate((dkv0, dkv1, dkv2, dkv3)):
        for half in range(2):
            rows = slice(half * CHUNK, (half + 1) * CHUNK)
            at = source * 2 + half
            both = jnp.concatenate([dk_acc[at] * attention_scale, dv_acc[at]], axis=1)
            dkv[rows] = both.astype(bf16)


def attend_back(info, pos, q_t, near, kvs, out_t, logs, branch_blocks):
    return pl.pallas_call(
        attend_back_kernel,
        out_shape=(jax.ShapeDtypeStruct((3, HD, SPAN), bf16),)
        + (jax.ShapeDtypeStruct((SPAN, 2 * HD), bf16),) * 4,
        in_specs=[SCALARS] + vmem_specs(10 + GROUP),
        out_specs=tuple(vmem_specs(5)),
        scratch_shapes=[
            pltpu.VMEM((3, SPAN, HD), bf16),
            pltpu.VMEM((8, CHUNK, HD), bf16),
            pltpu.VMEM((8, HD, CHUNK), bf16),
            pltpu.VMEM((8, CHUNK, HD), bf16),
            pltpu.VMEM((3, HD, SPAN), bf16),
            pltpu.VMEM((3, SPAN, HD), bf16),
            pltpu.VMEM((3, HD, SPAN), f32),
            pltpu.VMEM((8, CHUNK, HD), f32),
            pltpu.VMEM((8, CHUNK, HD), f32),
            pltpu.VMEM((3, 1, SPAN), f32),
        ],
        compiler_params=pltpu.CompilerParams(vmem_limit_bytes=VMEM_LIMIT),
        cost_estimate=NO_COST,
        name="attend_back",
    )(info, pos[None, :], pos[:, None], q_t, near, *kvs, out_t, logs, *branch_blocks)


def turn_back_kernel(near_ref, tail_ref, cos_ref, sin_ref, dq_ref, kv0, kv1, kv2, kv3, *refs):
    xs = refs[:4]
    outs = refs[4 : 4 + GROUP]
    mixed_ref, gain_ref, back = refs[4 + GROUP :]
    kv_sum = kv0[...].astype(f32) + kv1[...].astype(f32) + kv2[...].astype(f32) + kv3[...].astype(f32)
    kv_sum = kv_sum.astype(bf16).astype(f32).T
    cosine = cos_ref[...]
    sine = sin_ref[...]
    for head in range(4):
        part = dq_ref[head].astype(f32) if head < 3 else kv_sum[:HD]
        low = part[:HALF]
        high = part[HALF:]
        back[head * HD : head * HD + HALF] = low * cosine + high * sine
        back[head * HD + HALF : (head + 1) * HD] = high * cosine - low * sine
    back[4 * HD :] = kv_sum[HD:]
    mixed_ref[...] = back[...].T.astype(bf16)
    weights = near_ref[:, :, : QW + 2 * HD].reshape(D, QW + 2 * HD)
    gain = jnp.zeros((1, D), f32)
    for at in range(GROUP):
        span = slice(at * TOK, (at + 1) * TOK)
        normed_grad = dot(mixed_ref[span], weights, ((1,), (1,)))
        outs[at][...] = normed_grad.astype(bf16)
        rows = xs[at // 2][at % 2].astype(f32)
        gain = gain + jnp.sum(normed_grad * (rows * rms_scale(rows)), axis=0, keepdims=True)
    gain_ref[...] = gain


def turn_back(near, tail, cosine, sine, dq_t, kv_parts, token_pairs):
    return pl.pallas_call(
        turn_back_kernel,
        out_shape=(jax.ShapeDtypeStruct((TOK, D), bf16),) * GROUP
        + (jax.ShapeDtypeStruct((SPAN, QW + 2 * HD), bf16), jax.ShapeDtypeStruct((1, D), f32)),
        in_specs=vmem_specs(13),
        out_specs=tuple(vmem_specs(GROUP + 2)),
        scratch_shapes=[pltpu.VMEM((QW + 2 * HD, SPAN), f32)],
        compiler_params=pltpu.CompilerParams(vmem_limit_bytes=VMEM_LIMIT),
        cost_estimate=NO_COST,
        name="turn_back",
    )(near, tail, cosine, sine, dq_t, *kv_parts, *token_pairs)


def weight_grad_kernel(info_ref, normed_ref, mixed_ref, heads_ref, rest_ref, gain_ref, *refs):
    branches = refs[:GROUP]
    out_ref = refs[GROUP]
    in_grad = dot(normed_ref[...], mixed_ref[...], ((0,), (0,)))
    out_grad = jnp.zeros((384, QW), f32)
    for at in range(GROUP):
        heads = heads_ref[:, at * TOK : (at + 1) * TOK]
        out_grad = out_grad + dot(branches[at][...], heads, ((0,), (1,)))
    lane = lax.broadcasted_iota(jnp.int32, (384, 128), 1)
    column = jnp.broadcast_to(gain_ref[...], (128, 384)).T
    rest = jnp.where(lane == GAIN_AT, column, rest_ref[...])
    out_ref[0, 0, :, :, :320] = in_grad.astype(bf16).reshape(4, 96, 320)
    out_ref[0, 0, :, :, 320:384] = jnp.zeros((4, 96, 64), bf16)
    out_ref[0, 0, :, :, 384:512] = out_grad[:, :128].astype(bf16).reshape(4, 96, 128)
    last = jnp.concatenate([out_grad[:, 128:], rest[:, 64:]], axis=1)
    out_ref[0, 0, :, :, 512:] = last.astype(bf16).reshape(4, 96, 128)


def weight_grads(info, normed_all, mixed_grad, heads, rest, gain, branch_blocks):
    step = lambda r, zh, info: zh * 2 + jnp.bitwise_xor(info[3], r)
    fixed = lambda *shape: pl.BlockSpec(shape, lambda r, zh, info: (0,) * len(shape))
    return pl.pallas_call(
        weight_grad_kernel,
        grid_spec=pltpu.PrefetchScalarGridSpec(
            num_scalar_prefetch=1,
            grid=(2, 2),
            in_specs=[
                pl.BlockSpec((SPAN, 384), lambda r, zh, info: (0, step(r, zh, info))),
                fixed(SPAN, QW + 2 * HD),
                fixed(QW, SPAN),
                pl.BlockSpec((384, 128), lambda r, zh, info: (step(r, zh, info), 0)),
                pl.BlockSpec((1, 384), lambda r, zh, info: (0, step(r, zh, info))),
            ]
            + [pl.BlockSpec((TOK, 384), lambda r, zh, info: (0, step(r, zh, info)))] * GROUP,
            out_specs=pl.BlockSpec((1, 1, 4, 96, WIDE), lambda r, zh, info: (r, zh, 0, 0, 0)),
        ),
        out_shape=jax.ShapeDtypeStruct((2, 2, 4, 96, WIDE), bf16),
        compiler_params=pltpu.CompilerParams(vmem_limit_bytes=VMEM_LIMIT),
        cost_estimate=NO_COST,
        name="weight_grads",
    )(info, normed_all, mixed_grad, heads, rest, gain, *branch_blocks)


def token_grad_kernel(tail_ref, token_ref, hidden_ref, *refs):
    parts = refs[:4]
    out_ref = refs[4]
    normed_grad = total_of([part[...] for part in parts])
    rows = token_ref[...].astype(f32)
    gain = tail_ref[GAIN_AT : GAIN_AT + 1, :]
    out_ref[...] = hidden_ref[...] + norm_back(rows, rms_scale(rows), gain, normed_grad)


def token_grads(tail, tokens, hidden_grad, parts):
    return pl.pallas_call(
        token_grad_kernel,
        out_shape=jax.ShapeDtypeStruct((TOK, D), f32),
        in_specs=vmem_specs(7),
        out_specs=vmem_specs(1)[0],
        compiler_params=pltpu.CompilerParams(vmem_limit_bytes=VMEM_LIMIT),
        cost_estimate=NO_COST,
        name="token_grads",
    )(tail, tokens, hidden_grad, *parts)


def small_update_kernel(owned_ref, *refs):
    ins, outs, sums = refs[:12], refs[12:24], refs[24:]
    in_sum, out_sum = sums
    shared = jnp.zeros((12, 128), f32)
    for u in range(GROUP):
        grad = owned_ref[u].astype(f32)
        in_sum[:, u * QW : (u + 1) * QW] = grad[:, :QW]
        in_sum[:, 1536 + u * HD : 1536 + (u + 1) * HD] = grad[:, QW : QW + HD]
        in_sum[:, 2048 + u * HD : 2048 + (u + 1) * HD] = grad[:, QW + HD : QW + 2 * HD]
        out_sum[:, u * QW : (u + 1) * QW] = grad[:, 384 : 384 + QW]
        shared = shared + grad[:, 512:]
    square = jnp.concatenate([shared, jnp.zeros((116, 128), f32)], axis=0).T
    grads = (in_sum[...], out_sum[...], shared[:, ROUTER_AT : ROUTER_AT + EXPERTS], square[GAIN_AT : GAIN_AT + 2, :12])
    rates = (rate_project_in, rate_project_out, rate_router, rate_gains)
    for at in range(4):
        state = [ref[...] for ref in ins[at * 3 : at * 3 + 3]]
        for ref, new in zip(outs[at * 3 : at * 3 + 3], adam_update(*state, grads[at], rates[at])):
            ref[...] = new


def small_updates(owned, states):
    return pl.pallas_call(
        small_update_kernel,
        out_shape=tuple(jax.ShapeDtypeStruct(state.shape, f32) for state in states),
        in_specs=vmem_specs(13),
        out_specs=tuple(vmem_specs(12)),
        scratch_shapes=[pltpu.VMEM((12, 2560), f32), pltpu.VMEM((12, D), f32)],
        compiler_params=pltpu.CompilerParams(vmem_limit_bytes=VMEM_LIMIT),
        cost_estimate=NO_COST,
        name="small_updates",
    )(owned, *states)


def pick_rows(ranks):
    return ranks == lax.broadcasted_iota(jnp.int32, (CAP, TOK), 0)


def expert_kernel(info_ref, rank_ref, hit_ref, tail_ref, *refs):
    xs = refs[:GROUP]
    c_ref, w_ref, grad_ref, act_ref, both_ref, scale_ref, weighted_ref, gate_ref, rows, slots = refs[GROUP:]
    number = pl.program_id(0)

    @pl.when(number == 0)
    def _():
        router = tail_ref[...].astype(bf16)
        lane = lax.broadcasted_iota(jnp.int32, (CAP, 128), 1)
        for at in range(GROUP):
            span = slice(at * CAP, (at + 1) * CAP)
            logits = jnp.where(hit_ref[at] > 0.0, dot(xs[at][...], router, ((1,), (1,))), -jnp.inf)
            raised = jnp.exp(logits - jnp.max(logits, axis=1, keepdims=True))
            gates = raised / jnp.sum(raised, axis=1, keepdims=True)
            if at == 0:
                gate_ref[...] = gates
            high = gates.astype(bf16)
            low = (gates - high.astype(f32)).astype(bf16)
            hits = [pick_rows(rank_ref[e, at : at + 1, :]) for e in range(LOCAL_E)]
            onehot = jnp.concatenate(hits, axis=0).astype(f32).astype(bf16)
            x_rows = dot(onehot, xs[at][...], ((1,), (0,))).astype(bf16)
            cots = c_ref[jnp.bitwise_xor(info_ref[4], at // 2), at % 2, :, :D]
            c_rows = dot(onehot, cots, ((1,), (0,))) * residual_scale
            slot_gates = dot(onehot, high, ((1,), (0,))) + dot(onehot, low, ((1,), (0,)))
            for e in range(LOCAL_E):
                cut = slice(e * CAP, (e + 1) * CAP)
                rows[e, span] = x_rows[cut]
                mine = lane == ROUTER_AT + info_ref[2] * LOCAL_E + e
                scale = jnp.sum(jnp.where(mine, slot_gates[cut], 0.0), axis=1, keepdims=True)
                scale_ref[e, span] = jnp.broadcast_to(scale, (CAP, 128))
                slots[e, span] = (c_rows[cut] * scale).astype(bf16)

    up = w_ref[:, 0, :, : 2 * F].reshape(D, 2 * F)
    down = w_ref[:, 0, :, 2 * F :].reshape(D, F)
    both = dot(rows[number], up, ((1,), (0,)))
    gate = both[:, :F]
    linear = both[:, F:]
    sigmoid = 1.0 / (1.0 + jnp.exp(-gate))
    silu = gate * sigmoid
    activated = (silu * linear).astype(bf16)
    act_ref[0] = activated
    slope = sigmoid * (1.0 + gate * (1.0 - sigmoid))
    act_grad = dot(slots[number], down, ((1,), (0,)))
    weighted = jnp.sum(activated.astype(f32) * act_grad, axis=1, keepdims=True)
    weighted_ref[0] = jnp.broadcast_to(weighted, (SLOTS, 128))
    both_ref[0, :, :F] = (act_grad * linear * slope).astype(bf16)
    both_ref[0, :, F:] = (act_grad * silu).astype(bf16)
    for at in range(4):
        cols = slice(at * 384, (at + 1) * 384)
        up_grad = dot(rows[number, :, cols], both_ref[0], ((0,), (0,)))
        grad_ref[at * 4 : at * 4 + 4, 0, :, : 2 * F] = up_grad.astype(bf16).reshape(4, 96, 2 * F)
        down_grad = dot(slots[number, :, cols], act_ref[0], ((0,), (0,)))
        grad_ref[at * 4 : at * 4 + 4, 0, :, 2 * F :] = down_grad.astype(bf16).reshape(4, 96, F)


def whole(*shape):
    return pl.BlockSpec(shape, lambda e: (0,) * len(shape), pipeline_mode=pl.Buffered(1))


def per_expert(rows, columns):
    return pl.BlockSpec((1, rows, columns), lambda e: (e, 0, 0))


def expert_pass(info, ranks, hits, tail, rows, cots, weights):
    return pl.pallas_call(
        expert_kernel,
        grid=(LOCAL_E,),
        out_shape=(
            jax.ShapeDtypeStruct((16, LOCAL_E, 96, 3 * F), bf16),
            jax.ShapeDtypeStruct((LOCAL_E, SLOTS, F), bf16),
            jax.ShapeDtypeStruct((LOCAL_E, SLOTS, 2 * F), bf16),
            jax.ShapeDtypeStruct((LOCAL_E, SLOTS, 128), f32),
            jax.ShapeDtypeStruct((LOCAL_E, SLOTS, 128), f32),
            jax.ShapeDtypeStruct((TOK, 128), f32),
        ),
        in_specs=[SCALARS]
        + [whole(LOCAL_E, GROUP, TOK), whole(GROUP, TOK, 128), whole(128, D)]
        + [whole(TOK, D)] * GROUP
        + [whole(4, 2, TOK, D + EXTRA)]
        + [pl.BlockSpec((16, 1, 96, 3 * F), lambda e: (0, e, 0, 0))],
        out_specs=(
            pl.BlockSpec((16, 1, 96, 3 * F), lambda e: (0, e, 0, 0)),
            per_expert(SLOTS, F),
            per_expert(SLOTS, 2 * F),
            whole(LOCAL_E, SLOTS, 128),
            per_expert(SLOTS, 128),
            whole(TOK, 128),
        ),
        scratch_shapes=[pltpu.VMEM((LOCAL_E, SLOTS, D), bf16), pltpu.VMEM((LOCAL_E, SLOTS, D), bf16)],
        compiler_params=pltpu.CompilerParams(vmem_limit_bytes=VMEM_LIMIT),
        cost_estimate=NO_COST,
        name="experts",
    )(info, ranks, hits, tail, *rows, cots, weights)


def combine_blocks(rank_ref, held, outs):
    for at in range(GROUP):
        onehot = jnp.concatenate([pick_rows(rank_ref[e, at : at + 1, :]) for e in range(LOCAL_E)], axis=0)
        onehot = onehot.astype(f32).astype(bf16)
        outs[at][...] = dot(onehot, held[at], ((0,), (0,))).astype(bf16)


def input_grad_kernel(first_ref, rank_ref, both_ref, weighted_ref, w_ref, *refs):
    outs = refs[:GROUP]
    held = refs[GROUP]
    number = pl.program_id(0)
    up = w_ref[:, 0].reshape(D, 2 * F)
    back = dot(both_ref[0], up, ((1,), (1,))).astype(bf16)
    high = weighted_ref[0].astype(bf16).astype(f32)
    low = weighted_ref[0] - high
    lane = lax.broadcasted_iota(jnp.int32, (SLOTS, EXTRA), 1)
    mine = first_ref[0] + number
    tail = (jnp.where(lane == mine, high, 0.0) + jnp.where(lane == mine + EXPERTS, low, 0.0)).astype(bf16)
    for at in range(GROUP):
        span = slice(at * CAP, (at + 1) * CAP)
        place = pl.ds(pl.multiple_of(number * CAP, CAP), CAP)
        held[at, place, :D] = back[span]
        held[at, place, D:] = tail[span]

    @pl.when(number == LOCAL_E - 1)
    def _():
        combine_blocks(rank_ref, held, outs)


def expert_input_grads(first, ranks, both, weighted, weights):
    return pl.pallas_call(
        input_grad_kernel,
        grid=(LOCAL_E,),
        out_shape=(jax.ShapeDtypeStruct((TOK, D + EXTRA), bf16),) * GROUP,
        in_specs=[
            pl.BlockSpec(memory_space=pltpu.SMEM),
            whole(LOCAL_E, GROUP, TOK),
            per_expert(SLOTS, 2 * F),
            per_expert(SLOTS, 128),
            pl.BlockSpec((16, 1, 96, 2 * F), lambda e: (0, e, 0, 0)),
        ],
        out_specs=(whole(TOK, D + EXTRA),) * GROUP,
        scratch_shapes=[pltpu.VMEM((GROUP, LOCAL_E * CAP, D + EXTRA), bf16)],
        compiler_params=pltpu.CompilerParams(vmem_limit_bytes=VMEM_LIMIT),
        cost_estimate=NO_COST,
        name="input_grads",
    )(first, ranks, both, weighted, weights)


def mixture_kernel(info_ref, rank_ref, act_ref, scale_ref, w_ref, out_ref, held):
    number = pl.program_id(0)
    down = w_ref[:, 0].reshape(D, F)
    produced = dot(act_ref[0], down, ((1,), (1,))).astype(bf16).astype(f32)
    produced = (produced * scale_ref[0, :, 0:1]).astype(bf16)
    for at in range(GROUP):
        place = pl.ds(pl.multiple_of(number * CAP, CAP), CAP)
        held[at, place] = produced[at * CAP : (at + 1) * CAP]

    @pl.when(number == LOCAL_E - 1)
    def _():
        combine_blocks(rank_ref, held, [out_ref.at[jnp.bitwise_xor(info_ref[4], at // 2), at % 2] for at in range(GROUP)])


def expert_mixture(info, ranks, activated, scales, weights):
    return pl.pallas_call(
        mixture_kernel,
        grid=(LOCAL_E,),
        out_shape=jax.ShapeDtypeStruct((4, 2, TOK, D), bf16),
        in_specs=[
            SCALARS,
            whole(LOCAL_E, GROUP, TOK),
            per_expert(SLOTS, F),
            per_expert(SLOTS, 128),
            pl.BlockSpec((16, 1, 96, F), lambda e: (0, e, 0, 2)),
        ],
        out_specs=whole(4, 2, TOK, D),
        scratch_shapes=[pltpu.VMEM((GROUP, LOCAL_E * CAP, D), bf16)],
        compiler_params=pltpu.CompilerParams(vmem_limit_bytes=VMEM_LIMIT),
        cost_estimate=NO_COST,
        name="mixture",
    )(info, ranks, activated, scales, weights)


def shards(
    tokens, cotangent, routes, project_in, project_out, router_weight, norm_gains, expert_up, expert_down,
    project_in_first, project_in_second, project_out_first, project_out_second,
    router_weight_first, router_weight_second, norm_gains_first, norm_gains_second,
    expert_up_first, expert_up_second, expert_down_first, expert_down_second,
):
    block = lax.axis_index("blk")
    x_at = lax.axis_index("x")
    ulys = x_at * 2 + lax.axis_index("zl")

    experts_own = jnp.concatenate(
        [expert_up.astype(bf16), jnp.swapaxes(expert_down.astype(bf16), 1, 2)], axis=2
    )
    token_pair = jnp.stack([tokens, trade(tokens, "zl", 1)])
    token_pairs = [token_pair] + [trade(token_pair, "x", mask) for mask in (1, 2, 3)]

    core = lax.axis_index("co")
    info = jnp.stack([block, x_at // 2, ulys, core, x_at]).astype(jnp.int32)
    in_own = project_in.astype(bf16)
    shared = jnp.concatenate([router_weight.astype(bf16), norm_gains.astype(bf16).T], axis=1)
    shared = jnp.pad(shared, ((0, 0), (0, 22)))
    cut = lambda v: jnp.swapaxes(v.reshape(12, GROUP, -1), 0, 1)
    payload = jnp.concatenate(
        [
            cut(in_own[:, :1536]),
            cut(in_own[:, 1536:2048]),
            cut(in_own[:, 2048:]),
            jnp.zeros((GROUP, 12, 64), bf16),
            cut(project_out.astype(bf16).T),
            jnp.broadcast_to(shared[None], (GROUP, 12, 64)),
        ],
        axis=2,
    )
    near_rows = a2a(payload, ULYS).reshape(96, WIDE)
    carried = jnp.concatenate(
        [cotangent, jnp.pad(routes.astype(bf16), ((0, 0), (0, EXTRA - TOPK)))], axis=1
    )
    carried_partner = trade(after(carried, token_pair), "zl", 1)
    near_mine = a2a(jnp.broadcast_to(near_rows[None], (8, 96, WIDE)), ("zh", "blk"))
    near_other = trade(near_mine, "co", 1)
    experts_own = lax.optimization_barrier(
        (experts_own.reshape(LOCAL_E * 96, 3 * F), near_mine, carried_partner, *token_pairs)
    )[0]
    experts_full = lax.all_gather(experts_own, DPBLK, axis=0, tiled=True).reshape(16, LOCAL_E, 96, 3 * F)

    at_of = jnp.arange(SPAN, dtype=jnp.int32) // TOK
    within = ((ulys & 3) ^ (at_of & 3)) * TOK + jnp.arange(SPAN, dtype=jnp.int32) % TOK
    chunk_of = 2 * block + ((at_of // 4) ^ (x_at // 2))
    position = (chunk_of * CHUNK + within).astype(f32)
    frequency = rope_base ** (-jnp.arange(HALF, dtype=f32) * 2.0 / HD)
    angles = frequency[:, None] * position[None, :]
    cosine = jnp.cos(angles)
    sine = jnp.sin(angles)
    near, tail, normed_all, q_t, kv_t = project(info, near_mine, near_other, cosine, sine, token_pairs)
    router_t = tail[ROUTER_AT : ROUTER_AT + EXPERTS]
    gain_attn = tail[GAIN_AT]
    gain_ffn = tail[GAIN_AT + 1]
    kvs = [kv_t] + [trade(kv_t, "blk", mask) for mask in (1, 2, 3)]
    carried_pair = jnp.stack([carried, after(carried_partner, q_t)])
    carried_all = a2a(jnp.broadcast_to(carried_pair[None], (4, 2, TOK, D + EXTRA)), "x")
    mask_pos = within[:CHUNK]
    heads_t, heads_low, logs, *branch_parts = attend(info, mask_pos, q_t, near, kvs)
    branch = total_of(collect(branch_parts, carried_all))

    x_own = tokens.astype(f32)
    hidden = x_own + residual_scale * branch
    scale_ffn = rms_scale(hidden)
    normed_ffn = (hidden * scale_ffn * gain_ffn).astype(bf16)
    ffn_blocks = spread(normed_ffn, trade(normed_ffn, "zl", 1))

    lane_ids = jnp.arange(128, dtype=jnp.int32) - ROUTER_AT
    route_all = jnp.take(carried_all[..., D : D + TOPK], x_at ^ jnp.arange(4), axis=0)
    route_all = route_all.reshape(GROUP, TOK, TOPK).astype(jnp.int32)
    hits_all = jnp.any(route_all[..., None] == lane_ids, axis=2)
    first = (ulys * LOCAL_E).astype(jnp.int32)
    hits_local = lax.dynamic_slice_in_dim(hits_all, first + ROUTER_AT, LOCAL_E, axis=2)
    earlier = jnp.tril(jnp.ones((TOK, TOK), bf16), -1)
    ranks = jnp.einsum("rt,stj->jsr", earlier, hits_local.astype(bf16), preferred_element_type=f32)
    ranks = jnp.where(jnp.transpose(hits_local, (2, 0, 1)), ranks.astype(jnp.int32), -1)
    expert_grad, activated, both_grad, slot_gates, weighted, gates_own = expert_pass(
        info, ranks, hits_all.astype(f32), tail, ffn_blocks, carried_all, experts_full
    )
    gates_own = gates_own[:, ROUTER_AT : ROUTER_AT + EXPERTS]
    expert_sum = lax.psum_scatter(
        expert_grad.reshape(16 * LOCAL_E * 96, 3 * F), DPBLK, scatter_dimension=0, tiled=True
    ).reshape(LOCAL_E, 96, 3 * F)
    ffn_sums = expert_input_grads(first.reshape(1), ranks, both_grad, weighted, experts_full)
    mixture_sums = expert_mixture(info, after(ranks, ffn_sums[0]), activated, slot_gates, experts_full)
    returned = total_of(collect(ffn_sums, mixture_sums))

    upstream = cotangent.astype(f32)
    weighted = returned[:, D : D + EXPERTS] + returned[:, D + EXPERTS : D + 2 * EXPERTS]
    logit_grad = weighted - gates_own * jnp.sum(weighted, axis=1, keepdims=True)
    ffn_grad = returned[:, :D] + jnp.dot(logit_grad, router_t, precision=lax.Precision.HIGHEST)
    router_grad = dot(normed_ffn, logit_grad.astype(bf16), ((0,), (0,)))
    gain_ffn_grad = jnp.sum(ffn_grad * hidden * scale_ffn, axis=0)
    hidden_grad = upstream + norm_back(hidden, scale_ffn, gain_ffn, ffn_grad)
    branch_grad = (residual_scale * hidden_grad).astype(bf16)
    branch_blocks = spread(branch_grad, trade(branch_grad, "zl", 1))

    rest = jnp.concatenate([jnp.zeros((D, ROUTER_AT), f32), router_grad, jnp.zeros((D, 1), f32), gain_ffn_grad[:, None]], axis=1)
    rest = jnp.pad(rest, ((0, 0), (0, 128 - GAIN_AT - 2)))
    branch_blocks = list(lax.optimization_barrier((*branch_blocks, rest))[:GROUP])
    dq_t, *dkv = attend_back(info, mask_pos, q_t, near, kvs, heads_t, logs, branch_blocks)
    kv_parts = [dkv[0]] + [trade(dkv[mask], "blk", mask) for mask in (1, 2, 3)]
    mixture_parts = a2a(lax.optimization_barrier((mixture_sums, *branch_blocks))[0], "x")
    mixture_pair = jnp.sum(after(mixture_parts, dq_t).astype(f32), axis=0)
    mixture_other = trade(mixture_pair[1].astype(bf16), "zl", 1)
    kv_parts[0] = after(kv_parts[0], mixture_pair)

    *normed_parts, mixed_grad, gain_attn_grad = turn_back(near, tail, cosine, sine, dq_t, kv_parts, token_pairs)
    layer_out = hidden + residual_scale * (mixture_pair[0] + mixture_other.astype(f32))
    normed_all, layer_out = lax.optimization_barrier((normed_all, layer_out))
    grads = weight_grads(info, normed_all, mixed_grad, heads_low, rest, gain_attn_grad, branch_blocks)
    both_cores = grads[0].astype(f32) + trade(grads[1], "co", 1).astype(f32)
    row_parts = a2a(both_cores.astype(bf16).reshape(8, 96, WIDE), ("zh", "blk"))
    tokens_grad = token_grads(tail, tokens, hidden_grad, collect(normed_parts, both_cores, row_parts))

    row_sum = jnp.sum(row_parts.astype(f32), axis=0).astype(bf16)
    up_sum = expert_sum[:, :, : 2 * F].astype(f32)
    down_sum = jnp.swapaxes(expert_sum[:, :, 2 * F :], 1, 2).astype(f32)
    up_state = adam_update(expert_up, expert_up_first, expert_up_second, up_sum, rate_expert_up)
    down_state = adam_update(expert_down, expert_down_first, expert_down_second, down_sum, rate_expert_down)
    row_sum, *expert_state = lax.optimization_barrier((row_sum, *up_state, *down_state))
    owned = a2a(row_sum.reshape(GROUP, 12, WIDE), ULYS)
    small_state = small_updates(
        owned,
        (
            project_in, project_in_first, project_in_second,
            project_out.T, project_out_first.T, project_out_second.T,
            router_weight, router_weight_first, router_weight_second,
            norm_gains, norm_gains_first, norm_gains_second,
        ),
    )
    out_state = [state.T for state in small_state[3:6]]
    return (layer_out, tokens_grad, *small_state[:3], *out_state, *small_state[6:], *expert_state)


def solution(mesh):
    fine = Mesh(mesh.devices.reshape(2, 2, 4, 4, 2), ALL)
    rows = P(ALL, None)
    cols = P(None, ALL)
    up = P(ULYS, DPBLK, None)
    down = P(ULYS, None, DPBLK)
    in_specs = (rows,) * 4 + (cols, rows, cols, up, down)
    in_specs += (rows,) * 2 + (cols,) * 2 + (rows,) * 2 + (cols,) * 2 + (up,) * 2 + (down,) * 2
    out_specs = (rows,) * 5 + (cols,) * 3 + (rows,) * 3 + (cols,) * 3 + (up,) * 3 + (down,) * 3
    return jax.shard_map(shards, mesh=fine, in_specs=in_specs, out_specs=out_specs, check_vma=False)
```

```python
import functools

import jax
import jax.numpy as jnp
from jax import lax
from jax.experimental import pallas as pl
from jax.experimental.pallas import tpu as pltpu
from jax.sharding import Mesh
from jax.sharding import PartitionSpec as P

D = 1536
HQ = 24
HK = 8
HD = 64
F = 512
EXPERTS = 40
TOPK = 8
ADAM_STEP = 10
CAP = 48
TOK = 128
GROUP = 8
LOCAL_E = 5
SPAN = 1024
ROWS = 80
CHUNK = 512
QW = 192
SLOTS = GROUP * CAP
HALF = HD // 2
EXTRA = 128
VMEM_LIMIT = 60 << 20
WIDE = 640
ROUTER_AT = 64
GAIN_AT = 104

bf16 = jnp.bfloat16
f32 = jnp.float32
attention_scale = 0.015625
residual_scale = 0.22
norm_epsilon = 1e-06
rope_base = 10000.0
beta_first = 0.9
beta_second = 0.95
adam_epsilon = 1e-08
weight_decay = 0.1
rate_project_in = 0.2
rate_project_out = 2.0
rate_router = 0.03
rate_gains = 0.5
rate_expert_up = 0.05
rate_expert_down = 2.0
log2_e = 1.4426950408889634

ULYS = ("x", "zl")
ALL = ("zh", "co", "blk", "x", "zl")
DPBLK = ("zh", "co", "blk")


def dot(a, b, dims):
    return lax.dot_general(a, b, ((dims[0], dims[1]), ((), ())), preferred_element_type=f32)


def rms_scale(rows_in):
    return lax.rsqrt(jnp.mean(rows_in * rows_in, axis=1, keepdims=True) + norm_epsilon)


def norm_back(rows_in, scale_in, gain_in, grad_in):
    weighted = grad_in * gain_in
    inner_sum = jnp.mean(weighted * rows_in, axis=1, keepdims=True)
    return scale_in * weighted - rows_in * (scale_in * scale_in * scale_in) * inner_sum


def adam_update(weight, first_moment, second, gradient, step_rate):
    first_new = beta_first * first_moment + (1.0 - beta_first) * gradient
    second_new = beta_second * second + (1.0 - beta_second) * gradient * gradient
    first_hat = first_new / (1.0 - beta_first**ADAM_STEP)
    second_hat = second_new / (1.0 - beta_second**ADAM_STEP)
    weight_new = weight - step_rate * (
        first_hat / (jnp.sqrt(second_hat) + adam_epsilon) + weight_decay * weight
    )
    return (weight_new, first_new, second_new)


def a2a(value, axes):
    return lax.all_to_all(value, axes, split_axis=0, concat_axis=0, tiled=True)


def trade(value, axis, mask):
    return lax.ppermute(value, axis, [(i, i ^ mask) for i in range(2 if axis in ("zl", "co", "zh") else 4)])


def causal_trade(value, mask, up):
    pairs = [(i, i ^ mask) for i in range(4) if (i < i ^ mask) == up]
    return lax.ppermute(value, "blk", pairs)


def after(value, *others):
    return lax.optimization_barrier((value,) + others)[0]


def spread(near, partner):
    a0 = trade(near, "x", 1)
    b0 = trade(near, "x", 3)
    far0 = trade(near, "x", 2)
    b1 = trade(partner, "x", 3)
    a1 = trade(partner, "x", 1)
    far1 = trade(partner, "x", 2)
    return [near, partner, a0, a1, far0, far1, b0, b1]


def collect(blocks, gate=None, last=None):
    to3 = trade(blocks[5], "x", 3)
    to1 = trade(blocks[4], "x", 1)
    got3_1 = trade(blocks[7], "x", 3)
    if gate is not None:
        to3, to1, _ = lax.optimization_barrier((to3, to1, gate))
    send1 = (blocks[3].astype(f32) + to3.astype(f32)).astype(bf16)
    got1_1 = trade(send1, "x", 1)
    send3 = (blocks[6].astype(f32) + to1.astype(f32)).astype(bf16)
    keep1, send3, got3_1 = lax.optimization_barrier((blocks[2], send3, got3_1))
    got1_0 = trade(keep1, "x", 1)
    got3_0 = trade(send3, "x", 3)
    if last is not None:
        got1_1 = after(got1_1, last)
    other = (blocks[1].astype(f32) + got1_1.astype(f32) + got3_1.astype(f32)).astype(bf16)
    other = trade(other, "zl", 1)
    return (blocks[0], got1_0, got3_0, other)


def total_of(parts):
    return sum(part.astype(f32) for part in parts)


def vmem_specs(count):
    return [pl.BlockSpec(memory_space=pltpu.VMEM)] * count


NO_COST = pl.CostEstimate(flops=0, bytes_accessed=0, transcendentals=0)
SCALARS = pl.BlockSpec(memory_space=pltpu.SMEM)


def project_kernel(info_ref, mine_ref, other_ref, cos_ref, sin_ref, *refs):
    xs = refs[:4]
    near_ref, tail_ref, normed_ref, q_ref, kv_ref, mixed = refs[4:]
    for zh in range(2):
        for blk in range(4):
            own = (zh * 2 + info_ref[3]) * 4 + blk
            far = (zh * 2 + 1 - info_ref[3]) * 4 + blk
            near_ref[own] = mine_ref[zh * 4 + blk]
            near_ref[far] = other_ref[zh * 4 + blk]
    near = near_ref[...].reshape(D, WIDE)
    tail_ref[...] = near[:, 512:].astype(f32).T
    gain = tail_ref[GAIN_AT : GAIN_AT + 1, :]
    weights = near[:, : QW + 2 * HD]
    for at in range(GROUP):
        span = slice(at * TOK, (at + 1) * TOK)
        rows = xs[at // 2][at % 2].astype(f32)
        normed = (rows * rms_scale(rows) * gain).astype(bf16)
        normed_ref[span] = normed
        mixed[:, span] = dot(normed, weights, ((1,), (0,))).T
    cosine = cos_ref[...]
    sine = sin_ref[...]
    for head in range(4):
        low = mixed[head * HD : head * HD + HALF]
        high = mixed[head * HD + HALF : (head + 1) * HD]
        low_out = (low * cosine - high * sine).astype(bf16)
        high_out = (high * cosine + low * sine).astype(bf16)
        if head < 3:
            q_ref[head, :HALF] = low_out
            q_ref[head, HALF:] = high_out
        else:
            kv_ref[:HALF] = low_out
            kv_ref[HALF:HD] = high_out
    kv_ref[HD:] = mixed[4 * HD :].astype(bf16)


def project(info, mine, other, cosine, sine, token_pairs):
    return pl.pallas_call(
        project_kernel,
        out_shape=(
            jax.ShapeDtypeStruct((16, 96, WIDE), bf16),
            jax.ShapeDtypeStruct((128, D), f32),
            jax.ShapeDtypeStruct((SPAN, D), bf16),
            jax.ShapeDtypeStruct((3, HD, SPAN), bf16),
            jax.ShapeDtypeStruct((2 * HD, SPAN), bf16),
        ),
        in_specs=[SCALARS] + vmem_specs(8),
        out_specs=tuple(vmem_specs(5)),
        scratch_shapes=[pltpu.VMEM((QW + 2 * HD, SPAN), f32)],
        compiler_params=pltpu.CompilerParams(vmem_limit_bytes=VMEM_LIMIT),
        cost_estimate=NO_COST,
        name="project",
    )(info, mine, other, cosine, sine, *token_pairs)


def chunk_place(info_ref, chunk):
    source = jnp.bitwise_xor(chunk // 2, info_ref[0])
    return source * 2 + jnp.bitwise_xor(chunk % 2, info_ref[1])


def causal_parts(info_ref, part):
    for half in range(2):
        last = 2 * info_ref[0] + jnp.bitwise_xor(half, info_ref[1])
        part(half, half, True)

        def step(chunk, carry):
            part(half, chunk_place(info_ref, chunk), False)
            return carry

        lax.fori_loop(0, last, step, 0)


def attend_kernel(
    info_ref, pos_row, pos_col, q_ref, near_ref, kv0, kv1, kv2, kv3, out_ref, low_ref, log_ref, *refs
):
    branches = refs[:GROUP]
    keys, vals, acc, peak = refs[GROUP:]
    for source, kv in enumerate((kv0, kv1, kv2, kv3)):
        for half in range(2):
            cols = slice(half * CHUNK, (half + 1) * CHUNK)
            keys[source * 2 + half] = kv[:HD, cols].T
            vals[source * 2 + half, :HD] = kv[HD:, cols]
            vals[source * 2 + half, HD:] = jnp.ones((ROWS - HD, CHUNK), bf16)

    def run(follow):
        def part(half, at, masked):
            cols = slice(half * CHUNK, (half + 1) * CHUNK)
            key = keys[at]
            val = vals[at]
            for head in range(3):
                scores = dot(key, q_ref[head, :, cols], ((1,), (0,))) * (attention_scale * log2_e)
                if masked:
                    scores = jnp.where(pos_col[...] <= pos_row[...], scores, -jnp.inf)
                    now = jnp.max(scores, axis=0, keepdims=True)
                elif follow:
                    now = jnp.maximum(peak[head, :, cols], jnp.max(scores, axis=0, keepdims=True))
                else:
                    now = peak[head, :, cols]
                grown = dot(val, jnp.exp2(scores - now).astype(bf16), ((1,), (0,)))
                if masked:
                    acc[head, :, cols] = grown
                elif follow:
                    acc[head, :, cols] = acc[head, :, cols] * jnp.exp2(peak[head, :, cols] - now) + grown
                else:
                    acc[head, :, cols] += grown
                if masked or follow:
                    peak[head, :, cols] = now

        causal_parts(info_ref, part)

    run(False)
    odd = jnp.where(jnp.abs(acc[...]) < 1e37, 0.0, 1.0)

    @pl.when(jnp.sum(odd) > 0.0)
    def _():
        run(True)

    for head in range(3):
        total = acc[head, HD : HD + 1]
        result = acc[head, :HD] / total
        out_ref[head] = result
        log_ref[head] = peak[head] + jnp.log2(total)
        low_ref[head * HD : (head + 1) * HD] = result.astype(bf16)
    out_cols = near_ref[:, :, 384 : 384 + QW].reshape(D, QW)
    for at in range(GROUP):
        heads = low_ref[:, at * TOK : (at + 1) * TOK]
        branches[at][...] = dot(heads, out_cols, ((0,), (1,))).astype(bf16)


def attend(info, pos, q_t, near, kvs):
    return pl.pallas_call(
        attend_kernel,
        out_shape=(
            jax.ShapeDtypeStruct((3, HD, SPAN), f32),
            jax.ShapeDtypeStruct((QW, SPAN), bf16),
            jax.ShapeDtypeStruct((3, 1, SPAN), f32),
        )
        + (jax.ShapeDtypeStruct((TOK, D), bf16),) * GROUP,
        in_specs=[SCALARS] + vmem_specs(8),
        out_specs=tuple(vmem_specs(3 + GROUP)),
        scratch_shapes=[
            pltpu.VMEM((8, CHUNK, HD), bf16),
            pltpu.VMEM((8, ROWS, CHUNK), bf16),
            pltpu.VMEM((3, ROWS, SPAN), f32),
            pltpu.VMEM((3, 1, SPAN), f32),
        ],
        compiler_params=pltpu.CompilerParams(vmem_limit_bytes=VMEM_LIMIT),
        cost_estimate=NO_COST,
        name="attend",
    )(info, pos[None, :], pos[:, None], q_t, near, *kvs)


def attend_back_kernel(
    info_ref, pos_row, pos_col, qt_ref, near_ref, kv0, kv1, kv2, kv3, out_ref, log_ref, *refs
):
    grads = refs[:GROUP]
    dq_ref, dkv0, dkv1, dkv2, dkv3, qn, kn, kt, vn, gt, gn, dq_acc, dk_acc, dv_acc, inner = refs[GROUP:]
    for source, kv in enumerate((kv0, kv1, kv2, kv3)):
        for half in range(2):
            cols = slice(half * CHUNK, (half + 1) * CHUNK)
            kt[source * 2 + half] = kv[:HD, cols]
            kn[source * 2 + half] = kv[:HD, cols].T
            vn[source * 2 + half] = kv[HD:, cols].T
    out_cols = near_ref[:, :, 384 : 384 + QW].reshape(D, QW)
    for at in range(GROUP):
        span = slice(at * TOK, (at + 1) * TOK)
        grad = dot(grads[at][...], out_cols, ((1,), (0,)))
        grad_t = grad.T
        for head in range(3):
            gn[head, span] = grad[:, head * HD : (head + 1) * HD].astype(bf16)
            gt[head, :, span] = grad_t[head * HD : (head + 1) * HD].astype(bf16)
    dk_acc[...] = jnp.zeros_like(dk_acc)
    dv_acc[...] = jnp.zeros_like(dv_acc)
    for head in range(3):
        inner[head] = jnp.sum(gt[head].astype(f32) * out_ref[head], axis=0, keepdims=True)
        qn[head] = qt_ref[head].T

    dq_acc[...] = jnp.zeros_like(dq_acc)

    def part(half, at, masked):
        cols = slice(half * CHUNK, (half + 1) * CHUNK)
        keys = kn[at]
        keys_t = kt[at]
        vals = vn[at]
        for head in range(3):
            scores = dot(keys, qt_ref[head, :, cols], ((1,), (0,))) * (attention_scale * log2_e)
            probs = jnp.exp2(scores - log_ref[head, :, cols])
            if masked:
                probs = jnp.where(pos_col[...] <= pos_row[...], probs, 0.0)
            prob_grad = dot(vals, gt[head, :, cols], ((1,), (0,)))
            score_grad = (probs * (prob_grad - inner[head, :, cols])).astype(bf16)
            dv_acc[at] += dot(probs.astype(bf16), gn[head, cols], ((1,), (0,)))
            dk_acc[at] += dot(score_grad, qn[head, cols], ((1,), (0,)))
            dq_acc[head, :, cols] += dot(keys_t, score_grad, ((1,), (0,)))

    causal_parts(info_ref, part)
    dq_ref[...] = (dq_acc[...] * attention_scale).astype(bf16)
    for source, dkv in enumerate((dkv0, dkv1, dkv2, dkv3)):
        for half in range(2):
            rows = slice(half * CHUNK, (half + 1) * CHUNK)
            at = source * 2 + half
            both = jnp.concatenate([dk_acc[at] * attention_scale, dv_acc[at]], axis=1)
            dkv[rows] = both.astype(bf16)


def attend_back(info, pos, q_t, near, kvs, out_t, logs, branch_blocks):
    return pl.pallas_call(
        attend_back_kernel,
        out_shape=(jax.ShapeDtypeStruct((3, HD, SPAN), bf16),)
        + (jax.ShapeDtypeStruct((SPAN, 2 * HD), bf16),) * 4,
        in_specs=[SCALARS] + vmem_specs(10 + GROUP),
        out_specs=tuple(vmem_specs(5)),
        scratch_shapes=[
            pltpu.VMEM((3, SPAN, HD), bf16),
            pltpu.VMEM((8, CHUNK, HD), bf16),
            pltpu.VMEM((8, HD, CHUNK), bf16),
            pltpu.VMEM((8, CHUNK, HD), bf16),
            pltpu.VMEM((3, HD, SPAN), bf16),
            pltpu.VMEM((3, SPAN, HD), bf16),
            pltpu.VMEM((3, HD, SPAN), f32),
            pltpu.VMEM((8, CHUNK, HD), f32),
            pltpu.VMEM((8, CHUNK, HD), f32),
            pltpu.VMEM((3, 1, SPAN), f32),
        ],
        compiler_params=pltpu.CompilerParams(vmem_limit_bytes=VMEM_LIMIT),
        cost_estimate=NO_COST,
        name="attend_back",
    )(info, pos[None, :], pos[:, None], q_t, near, *kvs, out_t, logs, *branch_blocks)


def turn_back_kernel(near_ref, tail_ref, cos_ref, sin_ref, dq_ref, kv0, kv1, kv2, kv3, *refs):
    xs = refs[:4]
    outs = refs[4 : 4 + GROUP]
    mixed_ref, gain_ref, back = refs[4 + GROUP :]
    kv_sum = kv0[...].astype(f32) + kv1[...].astype(f32) + kv2[...].astype(f32) + kv3[...].astype(f32)
    kv_sum = kv_sum.astype(bf16).astype(f32).T
    cosine = cos_ref[...]
    sine = sin_ref[...]
    for head in range(4):
        part = dq_ref[head].astype(f32) if head < 3 else kv_sum[:HD]
        low = part[:HALF]
        high = part[HALF:]
        back[head * HD : head * HD + HALF] = low * cosine + high * sine
        back[head * HD + HALF : (head + 1) * HD] = high * cosine - low * sine
    back[4 * HD :] = kv_sum[HD:]
    mixed_ref[...] = back[...].T.astype(bf16)
    weights = near_ref[:, :, : QW + 2 * HD].reshape(D, QW + 2 * HD)
    gain = jnp.zeros((1, D), f32)
    for at in range(GROUP):
        span = slice(at * TOK, (at + 1) * TOK)
        normed_grad = dot(mixed_ref[span], weights, ((1,), (1,)))
        outs[at][...] = normed_grad.astype(bf16)
        rows = xs[at // 2][at % 2].astype(f32)
        gain = gain + jnp.sum(normed_grad * (rows * rms_scale(rows)), axis=0, keepdims=True)
    gain_ref[...] = gain


def turn_back(near, tail, cosine, sine, dq_t, kv_parts, token_pairs):
    return pl.pallas_call(
        turn_back_kernel,
        out_shape=(jax.ShapeDtypeStruct((TOK, D), bf16),) * GROUP
        + (jax.ShapeDtypeStruct((SPAN, QW + 2 * HD), bf16), jax.ShapeDtypeStruct((1, D), f32)),
        in_specs=vmem_specs(13),
        out_specs=tuple(vmem_specs(GROUP + 2)),
        scratch_shapes=[pltpu.VMEM((QW + 2 * HD, SPAN), f32)],
        compiler_params=pltpu.CompilerParams(vmem_limit_bytes=VMEM_LIMIT),
        cost_estimate=NO_COST,
        name="turn_back",
    )(near, tail, cosine, sine, dq_t, *kv_parts, *token_pairs)


def weight_grad_kernel(info_ref, normed_ref, mixed_ref, heads_ref, rest_ref, gain_ref, *refs):
    branches = refs[:GROUP]
    out_ref = refs[GROUP]
    in_grad = dot(normed_ref[...], mixed_ref[...], ((0,), (0,)))
    out_grad = jnp.zeros((384, QW), f32)
    for at in range(GROUP):
        heads = heads_ref[:, at * TOK : (at + 1) * TOK]
        out_grad = out_grad + dot(branches[at][...], heads, ((0,), (1,)))
    lane = lax.broadcasted_iota(jnp.int32, (384, 128), 1)
    column = jnp.broadcast_to(gain_ref[...], (128, 384)).T
    rest = jnp.where(lane == GAIN_AT, column, rest_ref[...])
    out_ref[0, 0, :, :, :320] = in_grad.astype(bf16).reshape(4, 96, 320)
    out_ref[0, 0, :, :, 320:384] = jnp.zeros((4, 96, 64), bf16)
    out_ref[0, 0, :, :, 384:512] = out_grad[:, :128].astype(bf16).reshape(4, 96, 128)
    last = jnp.concatenate([out_grad[:, 128:], rest[:, 64:]], axis=1)
    out_ref[0, 0, :, :, 512:] = last.astype(bf16).reshape(4, 96, 128)


def weight_grads(info, normed_all, mixed_grad, heads, rest, gain, branch_blocks):
    step = lambda r, zh, info: zh * 2 + jnp.bitwise_xor(info[3], r)
    fixed = lambda *shape: pl.BlockSpec(shape, lambda r, zh, info: (0,) * len(shape))
    return pl.pallas_call(
        weight_grad_kernel,
        grid_spec=pltpu.PrefetchScalarGridSpec(
            num_scalar_prefetch=1,
            grid=(2, 2),
            in_specs=[
                pl.BlockSpec((SPAN, 384), lambda r, zh, info: (0, step(r, zh, info))),
                fixed(SPAN, QW + 2 * HD),
                fixed(QW, SPAN),
                pl.BlockSpec((384, 128), lambda r, zh, info: (step(r, zh, info), 0)),
                pl.BlockSpec((1, 384), lambda r, zh, info: (0, step(r, zh, info))),
            ]
            + [pl.BlockSpec((TOK, 384), lambda r, zh, info: (0, step(r, zh, info)))] * GROUP,
            out_specs=pl.BlockSpec((1, 1, 4, 96, WIDE), lambda r, zh, info: (r, zh, 0, 0, 0)),
        ),
        out_shape=jax.ShapeDtypeStruct((2, 2, 4, 96, WIDE), bf16),
        compiler_params=pltpu.CompilerParams(vmem_limit_bytes=VMEM_LIMIT),
        cost_estimate=NO_COST,
        name="weight_grads",
    )(info, normed_all, mixed_grad, heads, rest, gain, *branch_blocks)


def token_grad_kernel(tail_ref, token_ref, hidden_ref, *refs):
    parts = refs[:4]
    out_ref = refs[4]
    normed_grad = total_of([part[...] for part in parts])
    rows = token_ref[...].astype(f32)
    gain = tail_ref[GAIN_AT : GAIN_AT + 1, :]
    out_ref[...] = hidden_ref[...] + norm_back(rows, rms_scale(rows), gain, normed_grad)


def token_grads(tail, tokens, hidden_grad, parts):
    return pl.pallas_call(
        token_grad_kernel,
        out_shape=jax.ShapeDtypeStruct((TOK, D), f32),
        in_specs=vmem_specs(7),
        out_specs=vmem_specs(1)[0],
        compiler_params=pltpu.CompilerParams(vmem_limit_bytes=VMEM_LIMIT),
        cost_estimate=NO_COST,
        name="token_grads",
    )(tail, tokens, hidden_grad, *parts)


def small_update_kernel(owned_ref, *refs):
    ins, outs, sums = refs[:12], refs[12:24], refs[24:]
    in_sum, out_sum = sums
    shared = jnp.zeros((12, 128), f32)
    for u in range(GROUP):
        grad = owned_ref[u].astype(f32)
        in_sum[:, u * QW : (u + 1) * QW] = grad[:, :QW]
        in_sum[:, 1536 + u * HD : 1536 + (u + 1) * HD] = grad[:, QW : QW + HD]
        in_sum[:, 2048 + u * HD : 2048 + (u + 1) * HD] = grad[:, QW + HD : QW + 2 * HD]
        out_sum[:, u * QW : (u + 1) * QW] = grad[:, 384 : 384 + QW]
        shared = shared + grad[:, 512:]
    square = jnp.concatenate([shared, jnp.zeros((116, 128), f32)], axis=0).T
    grads = (in_sum[...], out_sum[...], shared[:, ROUTER_AT : ROUTER_AT + EXPERTS], square[GAIN_AT : GAIN_AT + 2, :12])
    rates = (rate_project_in, rate_project_out, rate_router, rate_gains)
    for at in range(4):
        state = [ref[...] for ref in ins[at * 3 : at * 3 + 3]]
        for ref, new in zip(outs[at * 3 : at * 3 + 3], adam_update(*state, grads[at], rates[at])):
            ref[...] = new


def small_updates(owned, states):
    return pl.pallas_call(
        small_update_kernel,
        out_shape=tuple(jax.ShapeDtypeStruct(state.shape, f32) for state in states),
        in_specs=vmem_specs(13),
        out_specs=tuple(vmem_specs(12)),
        scratch_shapes=[pltpu.VMEM((12, 2560), f32), pltpu.VMEM((12, D), f32)],
        compiler_params=pltpu.CompilerParams(vmem_limit_bytes=VMEM_LIMIT),
        cost_estimate=NO_COST,
        name="small_updates",
    )(owned, *states)


def pick_rows(ranks):
    return ranks == lax.broadcasted_iota(jnp.int32, (CAP, TOK), 0)


def expert_kernel(info_ref, rank_ref, hit_ref, tail_ref, *refs):
    xs = refs[:GROUP]
    c_ref, w_ref, grad_ref, act_ref, both_ref, scale_ref, weighted_ref, gate_ref, rows, slots = refs[GROUP:]
    number = pl.program_id(0)

    @pl.when(number == 0)
    def _():
        router = tail_ref[...].astype(bf16)
        lane = lax.broadcasted_iota(jnp.int32, (CAP, 128), 1)
        for at in range(GROUP):
            span = slice(at * CAP, (at + 1) * CAP)
            logits = jnp.where(hit_ref[at] > 0.0, dot(xs[at][...], router, ((1,), (1,))), -jnp.inf)
            raised = jnp.exp(logits - jnp.max(logits, axis=1, keepdims=True))
            gates = raised / jnp.sum(raised, axis=1, keepdims=True)
            if at == 0:
                gate_ref[...] = gates
            high = gates.astype(bf16)
            low = (gates - high.astype(f32)).astype(bf16)
            hits = [pick_rows(rank_ref[e, at : at + 1, :]) for e in range(LOCAL_E)]
            onehot = jnp.concatenate(hits, axis=0).astype(f32).astype(bf16)
            x_rows = dot(onehot, xs[at][...], ((1,), (0,))).astype(bf16)
            cots = c_ref[jnp.bitwise_xor(info_ref[4], at // 2), at % 2, :, :D]
            c_rows = dot(onehot, cots, ((1,), (0,))) * residual_scale
            slot_gates = dot(onehot, high, ((1,), (0,))) + dot(onehot, low, ((1,), (0,)))
            for e in range(LOCAL_E):
                cut = slice(e * CAP, (e + 1) * CAP)
                rows[e, span] = x_rows[cut]
                mine = lane == ROUTER_AT + info_ref[2] * LOCAL_E + e
                scale = jnp.sum(jnp.where(mine, slot_gates[cut], 0.0), axis=1, keepdims=True)
                scale_ref[e, span] = jnp.broadcast_to(scale, (CAP, 128))
                slots[e, span] = (c_rows[cut] * scale).astype(bf16)

    up = w_ref[:, 0, :, : 2 * F].reshape(D, 2 * F)
    down = w_ref[:, 0, :, 2 * F :].reshape(D, F)
    both = dot(rows[number], up, ((1,), (0,)))
    gate = both[:, :F]
    linear = both[:, F:]
    sigmoid = 1.0 / (1.0 + jnp.exp(-gate))
    silu = gate * sigmoid
    activated = (silu * linear).astype(bf16)
    act_ref[0] = activated
    slope = sigmoid * (1.0 + gate * (1.0 - sigmoid))
    act_grad = dot(slots[number], down, ((1,), (0,)))
    weighted = jnp.sum(activated.astype(f32) * act_grad, axis=1, keepdims=True)
    weighted_ref[0] = jnp.broadcast_to(weighted, (SLOTS, 128))
    both_ref[0, :, :F] = (act_grad * linear * slope).astype(bf16)
    both_ref[0, :, F:] = (act_grad * silu).astype(bf16)
    for at in range(4):
        cols = slice(at * 384, (at + 1) * 384)
        up_grad = dot(rows[number, :, cols], both_ref[0], ((0,), (0,)))
        grad_ref[at * 4 : at * 4 + 4, 0, :, : 2 * F] = up_grad.astype(bf16).reshape(4, 96, 2 * F)
        down_grad = dot(slots[number, :, cols], act_ref[0], ((0,), (0,)))
        grad_ref[at * 4 : at * 4 + 4, 0, :, 2 * F :] = down_grad.astype(bf16).reshape(4, 96, F)


def whole(*shape):
    return pl.BlockSpec(shape, lambda e: (0,) * len(shape), pipeline_mode=pl.Buffered(1))


def per_expert(rows, columns):
    return pl.BlockSpec((1, rows, columns), lambda e: (e, 0, 0))


def expert_pass(info, ranks, hits, tail, rows, cots, weights):
    return pl.pallas_call(
        expert_kernel,
        grid=(LOCAL_E,),
        out_shape=(
            jax.ShapeDtypeStruct((16, LOCAL_E, 96, 3 * F), bf16),
            jax.ShapeDtypeStruct((LOCAL_E, SLOTS, F), bf16),
            jax.ShapeDtypeStruct((LOCAL_E, SLOTS, 2 * F), bf16),
            jax.ShapeDtypeStruct((LOCAL_E, SLOTS, 128), f32),
            jax.ShapeDtypeStruct((LOCAL_E, SLOTS, 128), f32),
            jax.ShapeDtypeStruct((TOK, 128), f32),
        ),
        in_specs=[SCALARS]
        + [whole(LOCAL_E, GROUP, TOK), whole(GROUP, TOK, 128), whole(128, D)]
        + [whole(TOK, D)] * GROUP
        + [whole(4, 2, TOK, D + EXTRA)]
        + [pl.BlockSpec((16, 1, 96, 3 * F), lambda e: (0, e, 0, 0))],
        out_specs=(
            pl.BlockSpec((16, 1, 96, 3 * F), lambda e: (0, e, 0, 0)),
            per_expert(SLOTS, F),
            per_expert(SLOTS, 2 * F),
            whole(LOCAL_E, SLOTS, 128),
            per_expert(SLOTS, 128),
            whole(TOK, 128),
        ),
        scratch_shapes=[pltpu.VMEM((LOCAL_E, SLOTS, D), bf16), pltpu.VMEM((LOCAL_E, SLOTS, D), bf16)],
        compiler_params=pltpu.CompilerParams(vmem_limit_bytes=VMEM_LIMIT),
        cost_estimate=NO_COST,
        name="experts",
    )(info, ranks, hits, tail, *rows, cots, weights)


def combine_blocks(rank_ref, held, outs):
    for at in range(GROUP):
        onehot = jnp.concatenate([pick_rows(rank_ref[e, at : at + 1, :]) for e in range(LOCAL_E)], axis=0)
        onehot = onehot.astype(f32).astype(bf16)
        outs[at][...] = dot(onehot, held[at], ((0,), (0,))).astype(bf16)


def input_grad_kernel(first_ref, rank_ref, both_ref, weighted_ref, w_ref, *refs):
    outs = refs[:GROUP]
    held = refs[GROUP]
    number = pl.program_id(0)
    up = w_ref[:, 0].reshape(D, 2 * F)
    back = dot(both_ref[0], up, ((1,), (1,))).astype(bf16)
    high = weighted_ref[0].astype(bf16).astype(f32)
    low = weighted_ref[0] - high
    lane = lax.broadcasted_iota(jnp.int32, (SLOTS, EXTRA), 1)
    mine = first_ref[0] + number
    tail = (jnp.where(lane == mine, high, 0.0) + jnp.where(lane == mine + EXPERTS, low, 0.0)).astype(bf16)
    for at in range(GROUP):
        span = slice(at * CAP, (at + 1) * CAP)
        place = pl.ds(pl.multiple_of(number * CAP, CAP), CAP)
        held[at, place, :D] = back[span]
        held[at, place, D:] = tail[span]

    @pl.when(number == LOCAL_E - 1)
    def _():
        combine_blocks(rank_ref, held, outs)


def expert_input_grads(first, ranks, both, weighted, weights):
    return pl.pallas_call(
        input_grad_kernel,
        grid=(LOCAL_E,),
        out_shape=(jax.ShapeDtypeStruct((TOK, D + EXTRA), bf16),) * GROUP,
        in_specs=[
            pl.BlockSpec(memory_space=pltpu.SMEM),
            whole(LOCAL_E, GROUP, TOK),
            per_expert(SLOTS, 2 * F),
            per_expert(SLOTS, 128),
            pl.BlockSpec((16, 1, 96, 2 * F), lambda e: (0, e, 0, 0)),
        ],
        out_specs=(whole(TOK, D + EXTRA),) * GROUP,
        scratch_shapes=[pltpu.VMEM((GROUP, LOCAL_E * CAP, D + EXTRA), bf16)],
        compiler_params=pltpu.CompilerParams(vmem_limit_bytes=VMEM_LIMIT),
        cost_estimate=NO_COST,
        name="input_grads",
    )(first, ranks, both, weighted, weights)


def mixture_kernel(info_ref, rank_ref, act_ref, scale_ref, w_ref, out_ref, held):
    number = pl.program_id(0)
    down = w_ref[:, 0].reshape(D, F)
    produced = dot(act_ref[0], down, ((1,), (1,))).astype(bf16).astype(f32)
    produced = (produced * scale_ref[0, :, 0:1]).astype(bf16)
    for at in range(GROUP):
        place = pl.ds(pl.multiple_of(number * CAP, CAP), CAP)
        held[at, place] = produced[at * CAP : (at + 1) * CAP]

    @pl.when(number == LOCAL_E - 1)
    def _():
        combine_blocks(rank_ref, held, [out_ref.at[jnp.bitwise_xor(info_ref[4], at // 2), at % 2] for at in range(GROUP)])


def expert_mixture(info, ranks, activated, scales, weights):
    return pl.pallas_call(
        mixture_kernel,
        grid=(LOCAL_E,),
        out_shape=jax.ShapeDtypeStruct((4, 2, TOK, D), bf16),
        in_specs=[
            SCALARS,
            whole(LOCAL_E, GROUP, TOK),
            per_expert(SLOTS, F),
            per_expert(SLOTS, 128),
            pl.BlockSpec((16, 1, 96, F), lambda e: (0, e, 0, 2)),
        ],
        out_specs=whole(4, 2, TOK, D),
        scratch_shapes=[pltpu.VMEM((GROUP, LOCAL_E * CAP, D), bf16)],
        compiler_params=pltpu.CompilerParams(vmem_limit_bytes=VMEM_LIMIT),
        cost_estimate=NO_COST,
        name="mixture",
    )(info, ranks, activated, scales, weights)


def shards(
    tokens, cotangent, routes, project_in, project_out, router_weight, norm_gains, expert_up, expert_down,
    project_in_first, project_in_second, project_out_first, project_out_second,
    router_weight_first, router_weight_second, norm_gains_first, norm_gains_second,
    expert_up_first, expert_up_second, expert_down_first, expert_down_second,
):
    block = lax.axis_index("blk")
    x_at = lax.axis_index("x")
    ulys = x_at * 2 + lax.axis_index("zl")

    experts_own = jnp.concatenate(
        [expert_up.astype(bf16), jnp.swapaxes(expert_down.astype(bf16), 1, 2)], axis=2
    )
    token_pair = jnp.stack([tokens, trade(tokens, "zl", 1)])
    token_pairs = [token_pair] + [trade(token_pair, "x", mask) for mask in (1, 2, 3)]

    core = lax.axis_index("co")
    info = jnp.stack([block, x_at // 2, ulys, core, x_at]).astype(jnp.int32)
    in_own = project_in.astype(bf16)
    shared = jnp.concatenate([router_weight.astype(bf16), norm_gains.astype(bf16).T], axis=1)
    shared = jnp.pad(shared, ((0, 0), (0, 22)))
    cut = lambda v: jnp.swapaxes(v.reshape(12, GROUP, -1), 0, 1)
    payload = jnp.concatenate(
        [
            cut(in_own[:, :1536]),
            cut(in_own[:, 1536:2048]),
            cut(in_own[:, 2048:]),
            jnp.zeros((GROUP, 12, 64), bf16),
            cut(project_out.astype(bf16).T),
            jnp.broadcast_to(shared[None], (GROUP, 12, 64)),
        ],
        axis=2,
    )
    near_rows = a2a(payload, ULYS).reshape(96, WIDE)
    carried = jnp.concatenate(
        [cotangent, jnp.pad(routes.astype(bf16), ((0, 0), (0, EXTRA - TOPK)))], axis=1
    )
    carried_partner = trade(after(carried, token_pair), "zl", 1)
    near_rows = after(near_rows, token_pair)
    near_mine = a2a(jnp.broadcast_to(near_rows[None], (8, 96, WIDE)), ("zh", "blk"))
    near_other = trade(lax.optimization_barrier((near_mine, carried_partner, *token_pairs))[0], "co", 1)
    experts_own = experts_own.reshape(LOCAL_E * 96, 3 * F)
    experts_full = lax.all_gather(experts_own, DPBLK, axis=0, tiled=True).reshape(16, LOCAL_E, 96, 3 * F)

    at_of = jnp.arange(SPAN, dtype=jnp.int32) // TOK
    within = ((ulys & 3) ^ (at_of & 3)) * TOK + jnp.arange(SPAN, dtype=jnp.int32) % TOK
    chunk_of = 2 * block + ((at_of // 4) ^ (x_at // 2))
    position = (chunk_of * CHUNK + within).astype(f32)
    frequency = rope_base ** (-jnp.arange(HALF, dtype=f32) * 2.0 / HD)
    angles = frequency[:, None] * position[None, :]
    cosine = jnp.cos(angles)
    sine = jnp.sin(angles)
    near, tail, normed_all, q_t, kv_t = project(info, near_mine, near_other, cosine, sine, token_pairs)
    router_t = tail[ROUTER_AT : ROUTER_AT + EXPERTS]
    gain_attn = tail[GAIN_AT]
    gain_ffn = tail[GAIN_AT + 1]
    kvs = [kv_t] + [causal_trade(kv_t, mask, True) for mask in (1, 2, 3)]
    carried_pair = jnp.stack([carried, after(carried_partner, q_t)])
    carried_all = a2a(jnp.broadcast_to(carried_pair[None], (4, 2, TOK, D + EXTRA)), "x")
    mask_pos = within[:CHUNK]
    heads_t, heads_low, logs, *branch_parts = attend(info, mask_pos, q_t, near, kvs)
    branch = total_of(collect(branch_parts, carried_all))

    x_own = tokens.astype(f32)
    hidden = x_own + residual_scale * branch
    scale_ffn = rms_scale(hidden)
    normed_ffn = (hidden * scale_ffn * gain_ffn).astype(bf16)
    ffn_blocks = spread(normed_ffn, trade(normed_ffn, "zl", 1))

    lane_ids = jnp.arange(128, dtype=jnp.int32) - ROUTER_AT
    route_all = jnp.take(carried_all[..., D : D + TOPK], x_at ^ jnp.arange(4), axis=0)
    route_all = route_all.reshape(GROUP, TOK, TOPK).astype(jnp.int32)
    hits_all = jnp.any(route_all[..., None] == lane_ids, axis=2)
    first = (ulys * LOCAL_E).astype(jnp.int32)
    hits_local = lax.dynamic_slice_in_dim(hits_all, first + ROUTER_AT, LOCAL_E, axis=2)
    earlier = jnp.tril(jnp.ones((TOK, TOK), bf16), -1)
    ranks = jnp.einsum("rt,stj->jsr", earlier, hits_local.astype(bf16), preferred_element_type=f32)
    ranks = jnp.where(jnp.transpose(hits_local, (2, 0, 1)), ranks.astype(jnp.int32), -1)
    expert_grad, activated, both_grad, slot_gates, weighted, gates_own = expert_pass(
        info, ranks, hits_all.astype(f32), tail, ffn_blocks, carried_all, experts_full
    )
    gates_own = gates_own[:, ROUTER_AT : ROUTER_AT + EXPERTS]
    expert_sum = lax.psum_scatter(
        expert_grad.reshape(16 * LOCAL_E * 96, 3 * F), DPBLK, scatter_dimension=0, tiled=True
    ).reshape(LOCAL_E, 96, 3 * F)
    ffn_sums = expert_input_grads(first.reshape(1), ranks, both_grad, weighted, experts_full)
    mixture_sums = expert_mixture(info, after(ranks, ffn_sums[0]), activated, slot_gates, experts_full)
    returned = total_of(collect(ffn_sums, mixture_sums))

    upstream = cotangent.astype(f32)
    weighted = returned[:, D : D + EXPERTS] + returned[:, D + EXPERTS : D + 2 * EXPERTS]
    logit_grad = weighted - gates_own * jnp.sum(weighted, axis=1, keepdims=True)
    ffn_grad = returned[:, :D] + jnp.dot(logit_grad, router_t, precision=lax.Precision.HIGHEST)
    router_grad = dot(normed_ffn, logit_grad.astype(bf16), ((0,), (0,)))
    gain_ffn_grad = jnp.sum(ffn_grad * hidden * scale_ffn, axis=0)
    hidden_grad = upstream + norm_back(hidden, scale_ffn, gain_ffn, ffn_grad)
    branch_grad = (residual_scale * hidden_grad).astype(bf16)
    branch_blocks = spread(branch_grad, trade(branch_grad, "zl", 1))

    rest = jnp.concatenate([jnp.zeros((D, ROUTER_AT), f32), router_grad, jnp.zeros((D, 1), f32), gain_ffn_grad[:, None]], axis=1)
    rest = jnp.pad(rest, ((0, 0), (0, 128 - GAIN_AT - 2)))
    branch_blocks = list(lax.optimization_barrier((*branch_blocks, rest))[:GROUP])
    dq_t, *dkv = attend_back(info, mask_pos, q_t, near, kvs, heads_t, logs, branch_blocks)
    kv_parts = [dkv[0]] + [causal_trade(dkv[mask], mask, False) for mask in (1, 2, 3)]
    mixture_parts = a2a(lax.optimization_barrier((mixture_sums, *branch_blocks))[0], "x")
    mixture_pair = jnp.sum(after(mixture_parts, dq_t).astype(f32), axis=0)
    mixture_other = trade(mixture_pair[1].astype(bf16), "zl", 1)
    kv_parts[0] = after(kv_parts[0], mixture_pair)

    *normed_parts, mixed_grad, gain_attn_grad = turn_back(near, tail, cosine, sine, dq_t, kv_parts, token_pairs)
    layer_out = hidden + residual_scale * (mixture_pair[0] + mixture_other.astype(f32))
    normed_all, layer_out = lax.optimization_barrier((normed_all, layer_out))
    grads = weight_grads(info, normed_all, mixed_grad, heads_low, rest, gain_attn_grad, branch_blocks)
    both_cores = grads[0].astype(f32) + trade(grads[1], "co", 1).astype(f32)
    row_parts = a2a(both_cores.astype(bf16).reshape(8, 96, WIDE), ("zh", "blk"))
    tokens_grad = token_grads(tail, tokens, hidden_grad, collect(normed_parts, both_cores, row_parts))

    row_sum = jnp.sum(row_parts.astype(f32), axis=0).astype(bf16)
    up_sum = expert_sum[:, :, : 2 * F].astype(f32)
    down_sum = jnp.swapaxes(expert_sum[:, :, 2 * F :], 1, 2).astype(f32)
    up_state = adam_update(expert_up, expert_up_first, expert_up_second, up_sum, rate_expert_up)
    down_state = adam_update(expert_down, expert_down_first, expert_down_second, down_sum, rate_expert_down)
    row_sum, *expert_state = lax.optimization_barrier((row_sum, *up_state, *down_state))
    owned = a2a(row_sum.reshape(GROUP, 12, WIDE), ULYS)
    small_state = small_updates(
        owned,
        (
            project_in, project_in_first, project_in_second,
            project_out.T, project_out_first.T, project_out_second.T,
            router_weight, router_weight_first, router_weight_second,
            norm_gains, norm_gains_first, norm_gains_second,
        ),
    )
    out_state = [state.T for state in small_state[3:6]]
    return (layer_out, tokens_grad, *small_state[:3], *out_state, *small_state[6:], *expert_state)


def solution(mesh):
    fine = Mesh(mesh.devices.reshape(2, 2, 4, 4, 2), ALL)
    rows = P(ALL, None)
    cols = P(None, ALL)
    up = P(ULYS, DPBLK, None)
    down = P(ULYS, None, DPBLK)
    in_specs = (rows,) * 4 + (cols, rows, cols, up, down)
    in_specs += (rows,) * 2 + (cols,) * 2 + (rows,) * 2 + (cols,) * 2 + (up,) * 2 + (down,) * 2
    out_specs = (rows,) * 5 + (cols,) * 3 + (rows,) * 3 + (cols,) * 3 + (up,) * 3 + (down,) * 3
    return jax.shard_map(shards, mesh=fine, in_specs=in_specs, out_specs=out_specs, check_vma=False)
```

```python
import functools

import jax
import jax.numpy as jnp
from jax import lax
from jax.experimental import pallas as pl
from jax.experimental.pallas import tpu as pltpu
from jax.sharding import Mesh
from jax.sharding import PartitionSpec as P

D = 1536
HQ = 24
HK = 8
HD = 64
F = 512
EXPERTS = 40
TOPK = 8
ADAM_STEP = 10
CAP = 48
TOK = 128
GROUP = 8
LOCAL_E = 5
SPAN = 1024
ROWS = 80
CHUNK = 512
QW = 192
SLOTS = GROUP * CAP
HALF = HD // 2
EXTRA = 128
VMEM_LIMIT = 60 << 20
WIDE = 640
ROUTER_AT = 64
GAIN_AT = 104

bf16 = jnp.bfloat16
f32 = jnp.float32
attention_scale = 0.015625
residual_scale = 0.22
norm_epsilon = 1e-06
rope_base = 10000.0
beta_first = 0.9
beta_second = 0.95
adam_epsilon = 1e-08
weight_decay = 0.1
rate_project_in = 0.2
rate_project_out = 2.0
rate_router = 0.03
rate_gains = 0.5
rate_expert_up = 0.05
rate_expert_down = 2.0
log2_e = 1.4426950408889634

ULYS = ("x", "zl")
ALL = ("zh", "co", "blk", "x", "zl")
DPBLK = ("zh", "co", "blk")


def dot(a, b, dims):
    return lax.dot_general(a, b, ((dims[0], dims[1]), ((), ())), preferred_element_type=f32)


def rms_scale(rows_in):
    return lax.rsqrt(jnp.mean(rows_in * rows_in, axis=1, keepdims=True) + norm_epsilon)


def norm_back(rows_in, scale_in, gain_in, grad_in):
    weighted = grad_in * gain_in
    inner_sum = jnp.mean(weighted * rows_in, axis=1, keepdims=True)
    return scale_in * weighted - rows_in * (scale_in * scale_in * scale_in) * inner_sum


def adam_update(weight, first_moment, second, gradient, step_rate):
    first_new = beta_first * first_moment + (1.0 - beta_first) * gradient
    second_new = beta_second * second + (1.0 - beta_second) * gradient * gradient
    first_hat = first_new / (1.0 - beta_first**ADAM_STEP)
    second_hat = second_new / (1.0 - beta_second**ADAM_STEP)
    weight_new = weight - step_rate * (
        first_hat / (jnp.sqrt(second_hat) + adam_epsilon) + weight_decay * weight
    )
    return (weight_new, first_new, second_new)


def a2a(value, axes):
    return lax.all_to_all(value, axes, split_axis=0, concat_axis=0, tiled=True)


def trade(value, axis, mask):
    return lax.ppermute(value, axis, [(i, i ^ mask) for i in range(2 if axis in ("zl", "co", "zh") else 4)])


def causal_trade(value, mask, up):
    pairs = [(i, i ^ mask) for i in range(4) if (i < i ^ mask) == up]
    return lax.ppermute(value, "blk", pairs)


def after(value, *others):
    return lax.optimization_barrier((value,) + others)[0]


def spread(near, partner):
    a0 = trade(near, "x", 1)
    b0 = trade(near, "x", 3)
    far0 = trade(near, "x", 2)
    b1 = trade(partner, "x", 3)
    a1 = trade(partner, "x", 1)
    far1 = trade(partner, "x", 2)
    return [near, partner, a0, a1, far0, far1, b0, b1]


def collect(blocks, gate=None, last=None):
    to3 = trade(blocks[5], "x", 3)
    to1 = trade(blocks[4], "x", 1)
    got3_1 = trade(blocks[7], "x", 3)
    if gate is not None:
        to3, to1, _ = lax.optimization_barrier((to3, to1, gate))
    send1 = (blocks[3].astype(f32) + to3.astype(f32)).astype(bf16)
    got1_1 = trade(send1, "x", 1)
    send3 = (blocks[6].astype(f32) + to1.astype(f32)).astype(bf16)
    keep1, send3, got3_1 = lax.optimization_barrier((blocks[2], send3, got3_1))
    got1_0 = trade(keep1, "x", 1)
    got3_0 = trade(send3, "x", 3)
    if last is not None:
        got1_1 = after(got1_1, last)
    other = (blocks[1].astype(f32) + got1_1.astype(f32) + got3_1.astype(f32)).astype(bf16)
    other = trade(other, "zl", 1)
    return (blocks[0], got1_0, got3_0, other)


def total_of(parts):
    return sum(part.astype(f32) for part in parts)


def vmem_specs(count):
    return [pl.BlockSpec(memory_space=pltpu.VMEM)] * count


NO_COST = pl.CostEstimate(flops=0, bytes_accessed=0, transcendentals=0)
SCALARS = pl.BlockSpec(memory_space=pltpu.SMEM)


def project_kernel(info_ref, mine_ref, other_ref, cos_ref, sin_ref, *refs):
    xs = refs[:4]
    near_ref, tail_ref, normed_ref, q_ref, kv_ref, mixed = refs[4:]
    for zh in range(2):
        for blk in range(4):
            own = (zh * 2 + info_ref[3]) * 4 + blk
            far = (zh * 2 + 1 - info_ref[3]) * 4 + blk
            near_ref[own] = mine_ref[zh * 4 + blk]
            near_ref[far] = other_ref[zh * 4 + blk]
    near = near_ref[...].reshape(D, WIDE)
    tail_ref[...] = near[:, 512:].astype(f32).T
    gain = tail_ref[GAIN_AT : GAIN_AT + 1, :]
    weights = near[:, : QW + 2 * HD]
    for at in range(GROUP):
        span = slice(at * TOK, (at + 1) * TOK)
        rows = xs[at // 2][at % 2].astype(f32)
        normed = (rows * rms_scale(rows) * gain).astype(bf16)
        normed_ref[span] = normed
        mixed[:, span] = dot(normed, weights, ((1,), (0,))).T
    cosine = cos_ref[...]
    sine = sin_ref[...]
    for head in range(4):
        low = mixed[head * HD : head * HD + HALF]
        high = mixed[head * HD + HALF : (head + 1) * HD]
        low_out = (low * cosine - high * sine).astype(bf16)
        high_out = (high * cosine + low * sine).astype(bf16)
        if head < 3:
            q_ref[head, :HALF] = low_out
            q_ref[head, HALF:] = high_out
        else:
            kv_ref[:HALF] = low_out
            kv_ref[HALF:HD] = high_out
    kv_ref[HD:] = mixed[4 * HD :].astype(bf16)


def project(info, mine, other, cosine, sine, token_pairs):
    return pl.pallas_call(
        project_kernel,
        out_shape=(
            jax.ShapeDtypeStruct((16, 96, WIDE), bf16),
            jax.ShapeDtypeStruct((128, D), f32),
            jax.ShapeDtypeStruct((SPAN, D), bf16),
            jax.ShapeDtypeStruct((3, HD, SPAN), bf16),
            jax.ShapeDtypeStruct((2 * HD, SPAN), bf16),
        ),
        in_specs=[SCALARS] + vmem_specs(8),
        out_specs=tuple(vmem_specs(5)),
        scratch_shapes=[pltpu.VMEM((QW + 2 * HD, SPAN), f32)],
        compiler_params=pltpu.CompilerParams(vmem_limit_bytes=VMEM_LIMIT),
        cost_estimate=NO_COST,
        name="project",
    )(info, mine, other, cosine, sine, *token_pairs)


def chunk_place(info_ref, chunk):
    source = jnp.bitwise_xor(chunk // 2, info_ref[0])
    return source * 2 + jnp.bitwise_xor(chunk % 2, info_ref[1])


def causal_parts(info_ref, part):
    for half in range(2):
        last = 2 * info_ref[0] + jnp.bitwise_xor(half, info_ref[1])
        part(half, half, True)

        def step(chunk, carry):
            part(half, chunk_place(info_ref, chunk), False)
            return carry

        lax.fori_loop(0, last, step, 0)


def attend_kernel(
    info_ref, pos_row, pos_col, q_ref, near_ref, kv0, kv1, kv2, kv3, out_ref, low_ref, log_ref, *refs
):
    branches = refs[:GROUP]
    keys, vals, acc, peak = refs[GROUP:]
    for source, kv in enumerate((kv0, kv1, kv2, kv3)):
        for half in range(2):
            cols = slice(half * CHUNK, (half + 1) * CHUNK)
            keys[source * 2 + half] = kv[:HD, cols].T
            vals[source * 2 + half, :HD] = kv[HD:, cols]
            vals[source * 2 + half, HD:] = jnp.ones((ROWS - HD, CHUNK), bf16)

    def run(follow):
        def part(half, at, masked):
            cols = slice(half * CHUNK, (half + 1) * CHUNK)
            key = keys[at]
            val = vals[at]
            for head in range(3):
                scores = dot(key, q_ref[head, :, cols], ((1,), (0,))) * (attention_scale * log2_e)
                if masked:
                    scores = jnp.where(pos_col[...] <= pos_row[...], scores, -jnp.inf)
                    now = jnp.max(scores, axis=0, keepdims=True)
                elif follow:
                    now = jnp.maximum(peak[head, :, cols], jnp.max(scores, axis=0, keepdims=True))
                else:
                    now = peak[head, :, cols]
                grown = dot(val, jnp.exp2(scores - now).astype(bf16), ((1,), (0,)))
                if masked:
                    acc[head, :, cols] = grown
                elif follow:
                    acc[head, :, cols] = acc[head, :, cols] * jnp.exp2(peak[head, :, cols] - now) + grown
                else:
                    acc[head, :, cols] += grown
                if masked or follow:
                    peak[head, :, cols] = now

        causal_parts(info_ref, part)

    run(False)
    odd = jnp.where(jnp.abs(acc[...]) < 1e37, 0.0, 1.0)

    @pl.when(jnp.sum(odd) > 0.0)
    def _():
        run(True)

    for head in range(3):
        total = acc[head, HD : HD + 1]
        result = acc[head, :HD] / total
        out_ref[head] = result
        log_ref[head] = peak[head] + jnp.log2(total)
        low_ref[head * HD : (head + 1) * HD] = result.astype(bf16)
    out_cols = near_ref[:, :, 384 : 384 + QW].reshape(D, QW)
    for at in range(GROUP):
        heads = low_ref[:, at * TOK : (at + 1) * TOK]
        branches[at][...] = dot(heads, out_cols, ((0,), (1,))).astype(bf16)


def attend(info, pos, q_t, near, kvs):
    return pl.pallas_call(
        attend_kernel,
        out_shape=(
            jax.ShapeDtypeStruct((3, HD, SPAN), f32),
            jax.ShapeDtypeStruct((QW, SPAN), bf16),
            jax.ShapeDtypeStruct((3, 1, SPAN), f32),
        )
        + (jax.ShapeDtypeStruct((TOK, D), bf16),) * GROUP,
        in_specs=[SCALARS] + vmem_specs(8),
        out_specs=tuple(vmem_specs(3 + GROUP)),
        scratch_shapes=[
            pltpu.VMEM((8, CHUNK, HD), bf16),
            pltpu.VMEM((8, ROWS, CHUNK), bf16),
            pltpu.VMEM((3, ROWS, SPAN), f32),
            pltpu.VMEM((3, 1, SPAN), f32),
        ],
        compiler_params=pltpu.CompilerParams(vmem_limit_bytes=VMEM_LIMIT),
        cost_estimate=NO_COST,
        name="attend",
    )(info, pos[None, :], pos[:, None], q_t, near, *kvs)


def attend_back_kernel(
    info_ref, pos_row, pos_col, qt_ref, near_ref, kv0, kv1, kv2, kv3, out_ref, log_ref, *refs
):
    grads = refs[:GROUP]
    dq_ref, dkv0, dkv1, dkv2, dkv3, qn, kn, kt, vn, gt, gn, dq_acc, dk_acc, dv_acc, inner = refs[GROUP:]
    for source, kv in enumerate((kv0, kv1, kv2, kv3)):
        for half in range(2):
            cols = slice(half * CHUNK, (half + 1) * CHUNK)
            kt[source * 2 + half] = kv[:HD, cols]
            kn[source * 2 + half] = kv[:HD, cols].T
            vn[source * 2 + half] = kv[HD:, cols].T
    out_cols = near_ref[:, :, 384 : 384 + QW].reshape(D, QW)
    for at in range(GROUP):
        span = slice(at * TOK, (at + 1) * TOK)
        grad = dot(grads[at][...], out_cols, ((1,), (0,)))
        grad_t = grad.T
        for head in range(3):
            gn[head, span] = grad[:, head * HD : (head + 1) * HD].astype(bf16)
            gt[head, :, span] = grad_t[head * HD : (head + 1) * HD].astype(bf16)
    dk_acc[...] = jnp.zeros_like(dk_acc)
    dv_acc[...] = jnp.zeros_like(dv_acc)
    for head in range(3):
        inner[head] = jnp.sum(gt[head].astype(f32) * out_ref[head], axis=0, keepdims=True)
        qn[head] = qt_ref[head].T

    dq_acc[...] = jnp.zeros_like(dq_acc)

    def part(half, at, masked):
        cols = slice(half * CHUNK, (half + 1) * CHUNK)
        keys = kn[at]
        keys_t = kt[at]
        vals = vn[at]
        for head in range(3):
            scores = dot(keys, qt_ref[head, :, cols], ((1,), (0,))) * (attention_scale * log2_e)
            probs = jnp.exp2(scores - log_ref[head, :, cols])
            if masked:
                probs = jnp.where(pos_col[...] <= pos_row[...], probs, 0.0)
            prob_grad = dot(vals, gt[head, :, cols], ((1,), (0,)))
            score_grad = (probs * (prob_grad - inner[head, :, cols])).astype(bf16)
            dv_acc[at] += dot(probs.astype(bf16), gn[head, cols], ((1,), (0,)))
            dk_acc[at] += dot(score_grad, qn[head, cols], ((1,), (0,)))
            dq_acc[head, :, cols] += dot(keys_t, score_grad, ((1,), (0,)))

    causal_parts(info_ref, part)
    dq_ref[...] = (dq_acc[...] * attention_scale).astype(bf16)
    for source, dkv in enumerate((dkv0, dkv1, dkv2, dkv3)):
        for half in range(2):
            rows = slice(half * CHUNK, (half + 1) * CHUNK)
            at = source * 2 + half
            both = jnp.concatenate([dk_acc[at] * attention_scale, dv_acc[at]], axis=1)
            dkv[rows] = both.astype(bf16)


def attend_back(info, pos, q_t, near, kvs, out_t, logs, branch_blocks):
    return pl.pallas_call(
        attend_back_kernel,
        out_shape=(jax.ShapeDtypeStruct((3, HD, SPAN), bf16),)
        + (jax.ShapeDtypeStruct((SPAN, 2 * HD), bf16),) * 4,
        in_specs=[SCALARS] + vmem_specs(10 + GROUP),
        out_specs=tuple(vmem_specs(5)),
        scratch_shapes=[
            pltpu.VMEM((3, SPAN, HD), bf16),
            pltpu.VMEM((8, CHUNK, HD), bf16),
            pltpu.VMEM((8, HD, CHUNK), bf16),
            pltpu.VMEM((8, CHUNK, HD), bf16),
            pltpu.VMEM((3, HD, SPAN), bf16),
            pltpu.VMEM((3, SPAN, HD), bf16),
            pltpu.VMEM((3, HD, SPAN), f32),
            pltpu.VMEM((8, CHUNK, HD), f32),
            pltpu.VMEM((8, CHUNK, HD), f32),
            pltpu.VMEM((3, 1, SPAN), f32),
        ],
        compiler_params=pltpu.CompilerParams(vmem_limit_bytes=VMEM_LIMIT),
        cost_estimate=NO_COST,
        name="attend_back",
    )(info, pos[None, :], pos[:, None], q_t, near, *kvs, out_t, logs, *branch_blocks)


def turn_back_kernel(near_ref, tail_ref, cos_ref, sin_ref, dq_ref, kv0, kv1, kv2, kv3, *refs):
    xs = refs[:4]
    outs = refs[4 : 4 + GROUP]
    mixed_ref, gain_ref, back = refs[4 + GROUP :]
    kv_sum = kv0[...].astype(f32) + kv1[...].astype(f32) + kv2[...].astype(f32) + kv3[...].astype(f32)
    kv_sum = kv_sum.astype(bf16).astype(f32).T
    cosine = cos_ref[...]
    sine = sin_ref[...]
    for head in range(4):
        part = dq_ref[head].astype(f32) if head < 3 else kv_sum[:HD]
        low = part[:HALF]
        high = part[HALF:]
        back[head * HD : head * HD + HALF] = low * cosine + high * sine
        back[head * HD + HALF : (head + 1) * HD] = high * cosine - low * sine
    back[4 * HD :] = kv_sum[HD:]
    mixed_ref[...] = back[...].T.astype(bf16)
    weights = near_ref[:, :, : QW + 2 * HD].reshape(D, QW + 2 * HD)
    gain = jnp.zeros((1, D), f32)
    for at in range(GROUP):
        span = slice(at * TOK, (at + 1) * TOK)
        normed_grad = dot(mixed_ref[span], weights, ((1,), (1,)))
        outs[at][...] = normed_grad.astype(bf16)
        rows = xs[at // 2][at % 2].astype(f32)
        gain = gain + jnp.sum(normed_grad * (rows * rms_scale(rows)), axis=0, keepdims=True)
    gain_ref[...] = gain


def turn_back(near, tail, cosine, sine, dq_t, kv_parts, token_pairs):
    return pl.pallas_call(
        turn_back_kernel,
        out_shape=(jax.ShapeDtypeStruct((TOK, D), bf16),) * GROUP
        + (jax.ShapeDtypeStruct((SPAN, QW + 2 * HD), bf16), jax.ShapeDtypeStruct((1, D), f32)),
        in_specs=vmem_specs(13),
        out_specs=tuple(vmem_specs(GROUP + 2)),
        scratch_shapes=[pltpu.VMEM((QW + 2 * HD, SPAN), f32)],
        compiler_params=pltpu.CompilerParams(vmem_limit_bytes=VMEM_LIMIT),
        cost_estimate=NO_COST,
        name="turn_back",
    )(near, tail, cosine, sine, dq_t, *kv_parts, *token_pairs)


def weight_grad_kernel(info_ref, normed_ref, mixed_ref, heads_ref, rest_ref, gain_ref, *refs):
    branches = refs[:GROUP]
    keep_ref, give_ref = refs[GROUP:]
    in_grad = dot(normed_ref[...], mixed_ref[...], ((0,), (0,)))
    out_grad = jnp.zeros((384, QW), f32)
    for at in range(GROUP):
        heads = heads_ref[:, at * TOK : (at + 1) * TOK]
        out_grad = out_grad + dot(branches[at][...], heads, ((0,), (1,)))
    lane = lax.broadcasted_iota(jnp.int32, (384, 128), 1)
    column = jnp.broadcast_to(gain_ref[...], (128, 384)).T
    rest = jnp.where(lane == GAIN_AT, column, rest_ref[...])
    last = jnp.concatenate([out_grad[:, 128:], rest[:, 64:]], axis=1)

    def write(out_ref):
        out_ref[0, :, :, :320] = in_grad.astype(bf16).reshape(4, 96, 320)
        out_ref[0, :, :, 320:384] = jnp.zeros((4, 96, 64), bf16)
        out_ref[0, :, :, 384:512] = out_grad[:, :128].astype(bf16).reshape(4, 96, 128)
        out_ref[0, :, :, 512:] = last.astype(bf16).reshape(4, 96, 128)

    @pl.when(pl.program_id(0) == 0)
    def _():
        write(keep_ref)

    @pl.when(pl.program_id(0) == 1)
    def _():
        write(give_ref)


def weight_grads(info, normed_all, mixed_grad, heads, rest, gain, branch_blocks):
    step = lambda r, zh, info: zh * 2 + jnp.bitwise_xor(info[3], r)
    fixed = lambda *shape: pl.BlockSpec(shape, lambda r, zh, info: (0,) * len(shape))
    return pl.pallas_call(
        weight_grad_kernel,
        grid_spec=pltpu.PrefetchScalarGridSpec(
            num_scalar_prefetch=1,
            grid=(2, 2),
            in_specs=[
                pl.BlockSpec((SPAN, 384), lambda r, zh, info: (0, step(r, zh, info))),
                fixed(SPAN, QW + 2 * HD),
                fixed(QW, SPAN),
                pl.BlockSpec((384, 128), lambda r, zh, info: (step(r, zh, info), 0)),
                pl.BlockSpec((1, 384), lambda r, zh, info: (0, step(r, zh, info))),
            ]
            + [pl.BlockSpec((TOK, 384), lambda r, zh, info: (0, step(r, zh, info)))] * GROUP,
            out_specs=(
                pl.BlockSpec((1, 4, 96, WIDE), lambda r, zh, info: (jnp.maximum(r, zh), 0, 0, 0)),
                pl.BlockSpec((1, 4, 96, WIDE), lambda r, zh, info: (r * zh, 0, 0, 0)),
            ),
        ),
        out_shape=(jax.ShapeDtypeStruct((2, 4, 96, WIDE), bf16),) * 2,
        compiler_params=pltpu.CompilerParams(vmem_limit_bytes=VMEM_LIMIT),
        cost_estimate=NO_COST,
        name="weight_grads",
    )(info, normed_all, mixed_grad, heads, rest, gain, *branch_blocks)


def token_grad_kernel(tail_ref, token_ref, hidden_ref, *refs):
    parts = refs[:4]
    out_ref = refs[4]
    normed_grad = total_of([part[...] for part in parts])
    rows = token_ref[...].astype(f32)
    gain = tail_ref[GAIN_AT : GAIN_AT + 1, :]
    out_ref[...] = hidden_ref[...] + norm_back(rows, rms_scale(rows), gain, normed_grad)


def token_grads(tail, tokens, hidden_grad, parts):
    return pl.pallas_call(
        token_grad_kernel,
        out_shape=jax.ShapeDtypeStruct((TOK, D), f32),
        in_specs=vmem_specs(7),
        out_specs=vmem_specs(1)[0],
        compiler_params=pltpu.CompilerParams(vmem_limit_bytes=VMEM_LIMIT),
        cost_estimate=NO_COST,
        name="token_grads",
    )(tail, tokens, hidden_grad, *parts)


def small_update_kernel(owned_ref, *refs):
    ins, outs, sums = refs[:12], refs[12:24], refs[24:]
    in_sum, out_sum = sums
    shared = jnp.zeros((12, 128), f32)
    for u in range(GROUP):
        grad = owned_ref[u].astype(f32)
        in_sum[:, u * QW : (u + 1) * QW] = grad[:, :QW]
        in_sum[:, 1536 + u * HD : 1536 + (u + 1) * HD] = grad[:, QW : QW + HD]
        in_sum[:, 2048 + u * HD : 2048 + (u + 1) * HD] = grad[:, QW + HD : QW + 2 * HD]
        out_sum[:, u * QW : (u + 1) * QW] = grad[:, 384 : 384 + QW]
        shared = shared + grad[:, 512:]
    square = jnp.concatenate([shared, jnp.zeros((116, 128), f32)], axis=0).T
    grads = (in_sum[...], out_sum[...], shared[:, ROUTER_AT : ROUTER_AT + EXPERTS], square[GAIN_AT : GAIN_AT + 2, :12])
    rates = (rate_project_in, rate_project_out, rate_router, rate_gains)
    for at in range(4):
        state = [ref[...] for ref in ins[at * 3 : at * 3 + 3]]
        for ref, new in zip(outs[at * 3 : at * 3 + 3], adam_update(*state, grads[at], rates[at])):
            ref[...] = new


def small_updates(owned, states):
    return pl.pallas_call(
        small_update_kernel,
        out_shape=tuple(jax.ShapeDtypeStruct(state.shape, f32) for state in states),
        in_specs=vmem_specs(13),
        out_specs=tuple(vmem_specs(12)),
        scratch_shapes=[pltpu.VMEM((12, 2560), f32), pltpu.VMEM((12, D), f32)],
        compiler_params=pltpu.CompilerParams(vmem_limit_bytes=VMEM_LIMIT),
        cost_estimate=NO_COST,
        name="small_updates",
    )(owned, *states)


def pick_rows(ranks):
    return ranks == lax.broadcasted_iota(jnp.int32, (CAP, TOK), 0)


def expert_kernel(info_ref, rank_ref, hit_ref, tail_ref, *refs):
    xs = refs[:GROUP]
    c_ref, w_ref, grad_ref, act_ref, both_ref, scale_ref, weighted_ref, gate_ref, rows, slots = refs[GROUP:]
    number = pl.program_id(0)

    @pl.when(number == 0)
    def _():
        router = tail_ref[...].astype(bf16)
        lane = lax.broadcasted_iota(jnp.int32, (CAP, 128), 1)
        for at in range(GROUP):
            span = slice(at * CAP, (at + 1) * CAP)
            logits = jnp.where(hit_ref[at] > 0.0, dot(xs[at][...], router, ((1,), (1,))), -jnp.inf)
            raised = jnp.exp(logits - jnp.max(logits, axis=1, keepdims=True))
            gates = raised / jnp.sum(raised, axis=1, keepdims=True)
            if at == 0:
                gate_ref[...] = gates
            high = gates.astype(bf16)
            low = (gates - high.astype(f32)).astype(bf16)
            hits = [pick_rows(rank_ref[e, at : at + 1, :]) for e in range(LOCAL_E)]
            onehot = jnp.concatenate(hits, axis=0).astype(f32).astype(bf16)
            x_rows = dot(onehot, xs[at][...], ((1,), (0,))).astype(bf16)
            cots = c_ref[jnp.bitwise_xor(info_ref[4], at // 2), at % 2, :, :D]
            c_rows = dot(onehot, cots, ((1,), (0,))) * residual_scale
            slot_gates = dot(onehot, high, ((1,), (0,))) + dot(onehot, low, ((1,), (0,)))
            for e in range(LOCAL_E):
                cut = slice(e * CAP, (e + 1) * CAP)
                rows[e, span] = x_rows[cut]
                mine = lane == ROUTER_AT + info_ref[2] * LOCAL_E + e
                scale = jnp.sum(jnp.where(mine, slot_gates[cut], 0.0), axis=1, keepdims=True)
                scale_ref[e, span] = jnp.broadcast_to(scale, (CAP, 128))
                slots[e, span] = (c_rows[cut] * scale).astype(bf16)

    up = w_ref[:, 0, :, : 2 * F].reshape(D, 2 * F)
    down = w_ref[:, 0, :, 2 * F :].reshape(D, F)
    both = dot(rows[number], up, ((1,), (0,)))
    gate = both[:, :F]
    linear = both[:, F:]
    sigmoid = 1.0 / (1.0 + jnp.exp(-gate))
    silu = gate * sigmoid
    activated = (silu * linear).astype(bf16)
    act_ref[0] = activated
    slope = sigmoid * (1.0 + gate * (1.0 - sigmoid))
    act_grad = dot(slots[number], down, ((1,), (0,)))
    weighted = jnp.sum(activated.astype(f32) * act_grad, axis=1, keepdims=True)
    weighted_ref[0] = jnp.broadcast_to(weighted, (SLOTS, 128))
    both_ref[0, :, :F] = (act_grad * linear * slope).astype(bf16)
    both_ref[0, :, F:] = (act_grad * silu).astype(bf16)
    for at in range(4):
        cols = slice(at * 384, (at + 1) * 384)
        up_grad = dot(rows[number, :, cols], both_ref[0], ((0,), (0,)))
        grad_ref[at * 4 : at * 4 + 4, 0, :, : 2 * F] = up_grad.astype(bf16).reshape(4, 96, 2 * F)
        down_grad = dot(slots[number, :, cols], act_ref[0], ((0,), (0,)))
        grad_ref[at * 4 : at * 4 + 4, 0, :, 2 * F :] = down_grad.astype(bf16).reshape(4, 96, F)


def whole(*shape):
    return pl.BlockSpec(shape, lambda e: (0,) * len(shape), pipeline_mode=pl.Buffered(1))


def per_expert(rows, columns):
    return pl.BlockSpec((1, rows, columns), lambda e: (e, 0, 0))


def expert_pass(info, ranks, hits, tail, rows, cots, weights):
    return pl.pallas_call(
        expert_kernel,
        grid=(LOCAL_E,),
        out_shape=(
            jax.ShapeDtypeStruct((16, LOCAL_E, 96, 3 * F), bf16),
            jax.ShapeDtypeStruct((LOCAL_E, SLOTS, F), bf16),
            jax.ShapeDtypeStruct((LOCAL_E, SLOTS, 2 * F), bf16),
            jax.ShapeDtypeStruct((LOCAL_E, SLOTS, 128), f32),
            jax.ShapeDtypeStruct((LOCAL_E, SLOTS, 128), f32),
            jax.ShapeDtypeStruct((TOK, 128), f32),
        ),
        in_specs=[SCALARS]
        + [whole(LOCAL_E, GROUP, TOK), whole(GROUP, TOK, 128), whole(128, D)]
        + [whole(TOK, D)] * GROUP
        + [whole(4, 2, TOK, D + EXTRA)]
        + [pl.BlockSpec((16, 1, 96, 3 * F), lambda e: (0, e, 0, 0))],
        out_specs=(
            pl.BlockSpec((16, 1, 96, 3 * F), lambda e: (0, e, 0, 0)),
            per_expert(SLOTS, F),
            per_expert(SLOTS, 2 * F),
            whole(LOCAL_E, SLOTS, 128),
            per_expert(SLOTS, 128),
            whole(TOK, 128),
        ),
        scratch_shapes=[pltpu.VMEM((LOCAL_E, SLOTS, D), bf16), pltpu.VMEM((LOCAL_E, SLOTS, D), bf16)],
        compiler_params=pltpu.CompilerParams(vmem_limit_bytes=VMEM_LIMIT),
        cost_estimate=NO_COST,
        name="experts",
    )(info, ranks, hits, tail, *rows, cots, weights)


def combine_blocks(rank_ref, held, outs):
    for at in range(GROUP):
        onehot = jnp.concatenate([pick_rows(rank_ref[e, at : at + 1, :]) for e in range(LOCAL_E)], axis=0)
        onehot = onehot.astype(f32).astype(bf16)
        outs[at][...] = dot(onehot, held[at], ((0,), (0,))).astype(bf16)


def input_grad_kernel(first_ref, rank_ref, both_ref, weighted_ref, w_ref, *refs):
    outs = refs[:GROUP]
    held = refs[GROUP]
    number = pl.program_id(0)
    up = w_ref[:, 0].reshape(D, 2 * F)
    back = dot(both_ref[0], up, ((1,), (1,))).astype(bf16)
    high = weighted_ref[0].astype(bf16).astype(f32)
    low = weighted_ref[0] - high
    lane = lax.broadcasted_iota(jnp.int32, (SLOTS, EXTRA), 1)
    mine = first_ref[0] + number
    tail = (jnp.where(lane == mine, high, 0.0) + jnp.where(lane == mine + EXPERTS, low, 0.0)).astype(bf16)
    for at in range(GROUP):
        span = slice(at * CAP, (at + 1) * CAP)
        place = pl.ds(pl.multiple_of(number * CAP, CAP), CAP)
        held[at, place, :D] = back[span]
        held[at, place, D:] = tail[span]

    @pl.when(number == LOCAL_E - 1)
    def _():
        combine_blocks(rank_ref, held, outs)


def expert_input_grads(first, ranks, both, weighted, weights):
    return pl.pallas_call(
        input_grad_kernel,
        grid=(LOCAL_E,),
        out_shape=(jax.ShapeDtypeStruct((TOK, D + EXTRA), bf16),) * GROUP,
        in_specs=[
            pl.BlockSpec(memory_space=pltpu.SMEM),
            whole(LOCAL_E, GROUP, TOK),
            per_expert(SLOTS, 2 * F),
            per_expert(SLOTS, 128),
            pl.BlockSpec((16, 1, 96, 2 * F), lambda e: (0, e, 0, 0)),
        ],
        out_specs=(whole(TOK, D + EXTRA),) * GROUP,
        scratch_shapes=[pltpu.VMEM((GROUP, LOCAL_E * CAP, D + EXTRA), bf16)],
        compiler_params=pltpu.CompilerParams(vmem_limit_bytes=VMEM_LIMIT),
        cost_estimate=NO_COST,
        name="input_grads",
    )(first, ranks, both, weighted, weights)


def mixture_kernel(info_ref, rank_ref, act_ref, scale_ref, w_ref, out_ref, held):
    number = pl.program_id(0)
    down = w_ref[:, 0].reshape(D, F)
    produced = dot(act_ref[0], down, ((1,), (1,))).astype(bf16).astype(f32)
    produced = (produced * scale_ref[0, :, 0:1]).astype(bf16)
    for at in range(GROUP):
        place = pl.ds(pl.multiple_of(number * CAP, CAP), CAP)
        held[at, place] = produced[at * CAP : (at + 1) * CAP]

    @pl.when(number == LOCAL_E - 1)
    def _():
        combine_blocks(rank_ref, held, [out_ref.at[jnp.bitwise_xor(info_ref[4], at // 2), at % 2] for at in range(GROUP)])


def expert_mixture(info, ranks, activated, scales, weights):
    return pl.pallas_call(
        mixture_kernel,
        grid=(LOCAL_E,),
        out_shape=jax.ShapeDtypeStruct((4, 2, TOK, D), bf16),
        in_specs=[
            SCALARS,
            whole(LOCAL_E, GROUP, TOK),
            per_expert(SLOTS, F),
            per_expert(SLOTS, 128),
            pl.BlockSpec((16, 1, 96, F), lambda e: (0, e, 0, 2)),
        ],
        out_specs=whole(4, 2, TOK, D),
        scratch_shapes=[pltpu.VMEM((GROUP, LOCAL_E * CAP, D), bf16)],
        compiler_params=pltpu.CompilerParams(vmem_limit_bytes=VMEM_LIMIT),
        cost_estimate=NO_COST,
        name="mixture",
    )(info, ranks, activated, scales, weights)


def shards(
    tokens, cotangent, routes, project_in, project_out, router_weight, norm_gains, expert_up, expert_down,
    project_in_first, project_in_second, project_out_first, project_out_second,
    router_weight_first, router_weight_second, norm_gains_first, norm_gains_second,
    expert_up_first, expert_up_second, expert_down_first, expert_down_second,
):
    block = lax.axis_index("blk")
    x_at = lax.axis_index("x")
    ulys = x_at * 2 + lax.axis_index("zl")

    experts_own = jnp.concatenate(
        [expert_up.astype(bf16), jnp.swapaxes(expert_down.astype(bf16), 1, 2)], axis=2
    )
    token_pair = jnp.stack([tokens, trade(tokens, "zl", 1)])
    token_pairs = [token_pair] + [trade(token_pair, "x", mask) for mask in (1, 2, 3)]

    core = lax.axis_index("co")
    info = jnp.stack([block, x_at // 2, ulys, core, x_at]).astype(jnp.int32)
    in_own = project_in.astype(bf16)
    shared = jnp.concatenate([router_weight.astype(bf16), norm_gains.astype(bf16).T], axis=1)
    shared = jnp.pad(shared, ((0, 0), (0, 22)))
    cut = lambda v: jnp.swapaxes(v.reshape(12, GROUP, -1), 0, 1)
    payload = jnp.concatenate(
        [
            cut(in_own[:, :1536]),
            cut(in_own[:, 1536:2048]),
            cut(in_own[:, 2048:]),
            jnp.zeros((GROUP, 12, 64), bf16),
            cut(project_out.astype(bf16).T),
            jnp.broadcast_to(shared[None], (GROUP, 12, 64)),
        ],
        axis=2,
    )
    near_rows = a2a(payload, ULYS).reshape(96, WIDE)
    carried = jnp.concatenate(
        [cotangent, jnp.pad(routes.astype(bf16), ((0, 0), (0, EXTRA - TOPK)))], axis=1
    )
    carried_partner = trade(after(carried, token_pair), "zl", 1)
    near_rows = after(near_rows, token_pair)
    near_mine = a2a(jnp.broadcast_to(near_rows[None], (8, 96, WIDE)), ("zh", "blk"))
    near_other = trade(lax.optimization_barrier((near_mine, carried_partner, *token_pairs))[0], "co", 1)
    experts_own = experts_own.reshape(LOCAL_E * 96, 3 * F)
    experts_full = lax.all_gather(experts_own, DPBLK, axis=0, tiled=True).reshape(16, LOCAL_E, 96, 3 * F)

    at_of = jnp.arange(SPAN, dtype=jnp.int32) // TOK
    within = ((ulys & 3) ^ (at_of & 3)) * TOK + jnp.arange(SPAN, dtype=jnp.int32) % TOK
    chunk_of = 2 * block + ((at_of // 4) ^ (x_at // 2))
    position = (chunk_of * CHUNK + within).astype(f32)
    frequency = rope_base ** (-jnp.arange(HALF, dtype=f32) * 2.0 / HD)
    angles = frequency[:, None] * position[None, :]
    cosine = jnp.cos(angles)
    sine = jnp.sin(angles)
    near, tail, normed_all, q_t, kv_t = project(info, near_mine, near_other, cosine, sine, token_pairs)
    router_t = tail[ROUTER_AT : ROUTER_AT + EXPERTS]
    gain_attn = tail[GAIN_AT]
    gain_ffn = tail[GAIN_AT + 1]
    kvs = [kv_t] + [causal_trade(kv_t, mask, True) for mask in (1, 2, 3)]
    carried_pair = jnp.stack([carried, after(carried_partner, q_t)])
    carried_all = a2a(jnp.broadcast_to(carried_pair[None], (4, 2, TOK, D + EXTRA)), "x")
    mask_pos = within[:CHUNK]
    heads_t, heads_low, logs, *branch_parts = attend(info, mask_pos, q_t, near, kvs)
    branch = total_of(collect(branch_parts, carried_all))

    x_own = tokens.astype(f32)
    hidden = x_own + residual_scale * branch
    scale_ffn = rms_scale(hidden)
    normed_ffn = (hidden * scale_ffn * gain_ffn).astype(bf16)
    ffn_blocks = spread(normed_ffn, trade(normed_ffn, "zl", 1))

    lane_ids = jnp.arange(128, dtype=jnp.int32) - ROUTER_AT
    route_all = jnp.take(carried_all[..., D : D + TOPK], x_at ^ jnp.arange(4), axis=0)
    route_all = route_all.reshape(GROUP, TOK, TOPK).astype(jnp.int32)
    hits_all = jnp.any(route_all[..., None] == lane_ids, axis=2)
    first = (ulys * LOCAL_E).astype(jnp.int32)
    hits_local = lax.dynamic_slice_in_dim(hits_all, first + ROUTER_AT, LOCAL_E, axis=2)
    earlier = jnp.tril(jnp.ones((TOK, TOK), bf16), -1)
    ranks = jnp.einsum("rt,stj->jsr", earlier, hits_local.astype(bf16), preferred_element_type=f32)
    ranks = jnp.where(jnp.transpose(hits_local, (2, 0, 1)), ranks.astype(jnp.int32), -1)
    expert_grad, activated, both_grad, slot_gates, weighted, gates_own = expert_pass(
        info, ranks, hits_all.astype(f32), tail, ffn_blocks, carried_all, experts_full
    )
    gates_own = gates_own[:, ROUTER_AT : ROUTER_AT + EXPERTS]
    expert_sum = lax.psum_scatter(
        expert_grad.reshape(16 * LOCAL_E * 96, 3 * F), DPBLK, scatter_dimension=0, tiled=True
    ).reshape(LOCAL_E, 96, 3 * F)
    ffn_sums = expert_input_grads(first.reshape(1), ranks, both_grad, weighted, experts_full)
    mixture_sums = expert_mixture(info, after(ranks, ffn_sums[0]), activated, slot_gates, experts_full)
    returned = total_of(collect(ffn_sums, mixture_sums))

    upstream = cotangent.astype(f32)
    weighted = returned[:, D : D + EXPERTS] + returned[:, D + EXPERTS : D + 2 * EXPERTS]
    logit_grad = weighted - gates_own * jnp.sum(weighted, axis=1, keepdims=True)
    ffn_grad = returned[:, :D] + jnp.dot(logit_grad, router_t, precision=lax.Precision.HIGHEST)
    router_grad = dot(normed_ffn, logit_grad.astype(bf16), ((0,), (0,)))
    gain_ffn_grad = jnp.sum(ffn_grad * hidden * scale_ffn, axis=0)
    hidden_grad = upstream + norm_back(hidden, scale_ffn, gain_ffn, ffn_grad)
    branch_grad = (residual_scale * hidden_grad).astype(bf16)
    branch_blocks = spread(branch_grad, trade(branch_grad, "zl", 1))

    rest = jnp.concatenate([jnp.zeros((D, ROUTER_AT), f32), router_grad, jnp.zeros((D, 1), f32), gain_ffn_grad[:, None]], axis=1)
    rest = jnp.pad(rest, ((0, 0), (0, 128 - GAIN_AT - 2)))
    branch_blocks = list(lax.optimization_barrier((*branch_blocks, rest))[:GROUP])
    dq_t, *dkv = attend_back(info, mask_pos, q_t, near, kvs, heads_t, logs, branch_blocks)
    kv_parts = [dkv[0]] + [causal_trade(dkv[mask], mask, False) for mask in (1, 2, 3)]
    mixture_parts = a2a(lax.optimization_barrier((mixture_sums, *branch_blocks))[0], "x")
    mixture_pair = jnp.sum(after(mixture_parts, dq_t).astype(f32), axis=0)
    mixture_other = trade(mixture_pair[1].astype(bf16), "zl", 1)
    kv_parts[0] = after(kv_parts[0], mixture_pair)

    *normed_parts, mixed_grad, gain_attn_grad = turn_back(near, tail, cosine, sine, dq_t, kv_parts, token_pairs)
    layer_out = hidden + residual_scale * (mixture_pair[0] + mixture_other.astype(f32))
    normed_all, layer_out = lax.optimization_barrier((normed_all, layer_out))
    keep, give = weight_grads(info, normed_all, mixed_grad, heads_low, rest, gain_attn_grad, branch_blocks)
    both_cores = keep.astype(f32) + trade(give, "co", 1).astype(f32)
    row_parts = a2a(both_cores.astype(bf16).reshape(8, 96, WIDE), ("zh", "blk"))
    tokens_grad = token_grads(tail, tokens, hidden_grad, collect(normed_parts, None, row_parts))

    row_sum = jnp.sum(row_parts.astype(f32), axis=0).astype(bf16)
    up_sum = expert_sum[:, :, : 2 * F].astype(f32)
    down_sum = jnp.swapaxes(expert_sum[:, :, 2 * F :], 1, 2).astype(f32)
    up_state = adam_update(expert_up, expert_up_first, expert_up_second, up_sum, rate_expert_up)
    down_state = adam_update(expert_down, expert_down_first, expert_down_second, down_sum, rate_expert_down)
    owned = a2a(row_sum.reshape(GROUP, 12, WIDE), ULYS)
    owned, *expert_state = lax.optimization_barrier((owned, *up_state, *down_state))
    small_state = small_updates(
        owned,
        (
            project_in, project_in_first, project_in_second,
            project_out.T, project_out_first.T, project_out_second.T,
            router_weight, router_weight_first, router_weight_second,
            norm_gains, norm_gains_first, norm_gains_second,
        ),
    )
    out_state = [state.T for state in small_state[3:6]]
    return (layer_out, tokens_grad, *small_state[:3], *out_state, *small_state[6:], *expert_state)


def solution(mesh):
    fine = Mesh(mesh.devices.reshape(2, 2, 4, 4, 2), ALL)
    rows = P(ALL, None)
    cols = P(None, ALL)
    up = P(ULYS, DPBLK, None)
    down = P(ULYS, None, DPBLK)
    in_specs = (rows,) * 4 + (cols, rows, cols, up, down)
    in_specs += (rows,) * 2 + (cols,) * 2 + (rows,) * 2 + (cols,) * 2 + (up,) * 2 + (down,) * 2
    out_specs = (rows,) * 5 + (cols,) * 3 + (rows,) * 3 + (cols,) * 3 + (up,) * 3 + (down,) * 3
    return jax.shard_map(shards, mesh=fine, in_specs=in_specs, out_specs=out_specs, check_vma=False)
```
